128 devices in a mesh: lat: 8 (over z, core), lon: 16 (over x, y).
Axes of the slice: x: 4, y: 4, z: 4, core: 2. Of those that a mesh axis runs over, the one named last changes fastest.
Arguments:
- runoff: bfloat16 [12, 1024, 4096], P(None, 'lat', 'lon'), may hold values from 0.049804688 to 2
- cell_order: int32 [8, 16, 32768], P('lat', 'lon'), may hold values from 0 to 32767, each once within a row
- map_weights: bfloat16 [8, 16, 256, 128, 128], P('lat', 'lon'), may hold values from 0 to 0.001953125
- dest_device: int32 [8, 16, 256, 1], replicated, may hold values from 0 to 127; in each aligned block of 256 rows (0 to 255, 256 to 511, ..., all dimensions but the last counted through in order) at most 4 rows name the same one
- dest_block: int32 [8, 16, 256], replicated, may hold values from 0 to 127
- initial_flow: float32 [8, 16, 128, 128], P('lat', 'lon'), may hold values from 0.2 to 1
- musk_k: float32 [8, 16, 128, 128], P('lat', 'lon'), may hold values from 2 to 120
- musk_x: float32 [8, 16, 128, 128], P('lat', 'lon'), may hold values from 0 to 0.3
- down_reach: int32 [8, 16, 128, 128], P('lat', 'lon'), may hold values from 1 to 128, as said below
- block_inverse: float32 [8, 16, 128, 128, 128], P('lat', 'lon'), as said below
- upstream_link: int32 [8, 16, 128], P('lat', 'lon'), may hold values from 0 to 127, each once within a row
Outputs:
- discharge: float32 [8, 16, 128, 128], P('lat', 'lon')
The draws below stay inside these ranges and needn't reach their ends.
Inputs may be any that keep to these rules, and one draw needn't show every extreme that they name: `cell_order`: each row of a device is a permutation of its 32768 cells. `dest_device`: at most 4 source blocks of one device name the same owner, and in every draw some device sends exactly 4 to some owner. `down_reach`: reach i of a block with 0 < i < 127 drains into a reach from i + 1 to 127; reach 0 drains into reach 127, and reach 127 holds 128. block_inverse of a block is the inverse of I - N diag(c1) of that block. `upstream_link`: each device's row is a permutation of its 128 blocks.
All inputs are finite; a program needn't handle non-finite values.
Results may differ from the reference program's by a relative error of at most 0.0003.
Values sent between devices are 32-bit elements; how exact they have to be, the bound alone decides.
No kernel may reach another device: no remote copies, remote signals or barrier semaphores. Data moves between devices by JAX's collectives and lax.ppermute only.
A program may use at most 128 MiB of HBM per device.

```python
import math
import jax
import jax.numpy as jnp
import numpy as np
from jax import lax

STEPS = 12
R = 128
CB = 128
CLAT = 128
CLON = 256
BLK = 128
CELLS = 32768
SRC = 256
SLOT = 4
NLAT = 1024
NLON = 4096
N_LAT = 8
N_LON = 16


substep_seconds = 300.0


def reach_tables(key):
    shape = (N_LAT, N_LON, BLK, R)
    position = lax.broadcasted_iota(jnp.int32, shape, 3)
    chooser = jax.random.randint(jax.random.fold_in(key, 101), shape, 0, 5)
    jump = jax.random.randint(jax.random.fold_in(key, 104), shape, 2, 4)
    stride = jnp.where(chooser < 4, 1, jump)
    drawn = jnp.minimum(position + stride, R - 1)
    drains = jnp.where(position == 0, R - 1, jnp.where(position == R - 1, R, drawn)).astype(jnp.int32)
    trunk = (position == 0) | (position == R - 1)
    spread_k = jax.random.uniform(jax.random.fold_in(key, 102), shape, jnp.float32)
    spread_x = jax.random.uniform(jax.random.fold_in(key, 103), shape, jnp.float32)
    trunk_high = 40.0
    inner_high = 120.0
    low = jnp.where(trunk, 2.0, 60.0)
    high = jnp.where(trunk, trunk_high, inner_high)
    travel = jnp.exp(jnp.log(low) + spread_k * (jnp.log(high) - jnp.log(low)))
    weighting = spread_x * jnp.where(trunk, 0.2, 0.3)
    half = 0.5 * substep_seconds
    first = (half - travel * weighting) / (travel * (1.0 - weighting) + half)
    reach_index = jnp.arange(R, dtype=jnp.int32)
    linkage = (drains[..., None, :] == reach_index[:, None]).astype(jnp.float32)
    power = first[..., None, :] * linkage
    inverse = jnp.eye(R, dtype=jnp.float32) + power
    for level in range(max(0, (R - 1).bit_length() - 1)):
        power = jnp.matmul(power, power, precision=lax.Precision.HIGHEST)
        inverse = inverse + jnp.matmul(inverse, power, precision=lax.Precision.HIGHEST)
    return (travel, weighting, drains, inverse)


def draw_musk_k(key, part):
    return reach_tables(key)[0]


def draw_musk_x(key, part):
    return reach_tables(key)[1]


def draw_down_reach(key, part):
    return reach_tables(key)[2]


def draw_block_inverse(key, part):
    return reach_tables(key)[3]


def plant(values, key, low, top_value):
    longest = values.shape.index(max(values.shape))
    spots = []
    for shift in (0, 1):
        where = [jax.random.randint(jax.random.fold_in(key, axis), (), 0, length) for axis, length in enumerate(values.shape)]
        where[longest] = (where[longest] + shift) % values.shape[longest]
        spots.append(tuple(where))
    return values.at[spots[0]].set(low).at[spots[1]].set(top_value)


def level_of(rng, extent, split, low, largest):
    def one(dim, shards_of):
        heights = jax.random.uniform(jax.random.fold_in(jax.random.fold_in(rng, 6), dim), (shards_of,), jnp.float32, low / len(split), largest / len(split))
        return jnp.repeat(jnp.exp(heights), extent[dim] // shards_of).reshape((-1,) + (1,) * (len(extent) - dim - 1))

    loudness = one(*split[0])
    for cut in split[1:]:
        loudness = loudness * one(*cut)
    return loudness


def deal_out(own_key, own, number, rows, amount, top, reach, skew):
    ranking = jax.random.permutation(own_key, amount)
    crowded, ordinary = shares(amount, rows * top, reach, skew, True), shares(amount, rows * top, reach, skew, False)
    places = jnp.arange(amount)

    def named(lengths, rotation):
        used = int((lengths > 0).sum())
        fixed = max(1, used // 4)
        moved = fixed + (places - fixed + rotation * (used - fixed)) % max(1, amount - fixed)
        return jnp.zeros((amount,), jnp.int32).at[ranking[jnp.where(places < fixed, places, moved)]].set(jnp.asarray(lengths, jnp.int32))

    lengths = jnp.where(number % 4 == 0, named(crowded, number // 4), named(ordinary, number - number // 4 - 1))
    mixed = jax.random.permutation(jax.random.fold_in(own, 3), amount)
    giver, taker = mixed[0:amount // 2 * 2:2], mixed[1:amount // 2 * 2:2]
    margin = jnp.minimum(lengths[giver] - 1, reach - lengths[taker]) // 2
    margin = jnp.where((giver == ranking[0]) | (taker == ranking[0]) | (lengths[taker] == 0), 0, jnp.maximum(margin, 0))
    moved = jax.random.randint(jax.random.fold_in(own, 4), (amount // 2,), 0, 1 << 20) % (margin + 1)
    lengths = lengths.at[giver].add(-moved).at[taker].add(moved)
    items = jnp.searchsorted(jnp.cumsum(lengths), jnp.arange(rows * top), side="right").astype(jnp.int32)
    listing = items.reshape(top, rows).T
    listing = listing[jax.random.permutation(jax.random.fold_in(own, 1), rows)]
    rotation = jax.random.randint(jax.random.fold_in(own, 2), (rows, 1), 0, top)
    return jnp.take_along_axis(listing, (jnp.arange(top)[None, :] + rotation) % top, axis=1)


def shares(count, total, reach, slope, full):
    loads = [(1 << 20) // math.isqrt(standing ** slope) + 1 for standing in range(1, count + 1)]
    largest = reach if full else min(reach, max(-(-total // count), total * loads[0] // sum(loads)))
    least = 1 if total - largest >= count - 1 else 0
    given, rest = [largest] + [least] * (count - 1), total - largest - least * (count - 1)
    while rest > 0:
        free = [i for i in range(1, count) if given[i] < largest] or [i for i in range(1, count) if given[i] < reach]
        whole, remaining = sum([loads[i] for i in free]), rest
        for i in free:
            extra = min(reach - given[i], max(1, remaining * loads[i] // whole), rest)
            given[i] = given[i] + extra
            rest = rest - extra
    return np.array(given)


def setup_inputs(seed: int = 0) -> dict:
    splits = jax.random.split(jax.random.key(seed), 12)
    runoff = jnp.clip(jnp.exp(math.log(2.0) - 3.6927934 * jax.random.uniform(splits[0], (STEPS, NLAT, NLON), jnp.float32) ** level_of(splits[0], (STEPS, NLAT, NLON), ((1, 8), (2, 16)), -0.2, 0.2)), 0.049804688, 2.0).astype(jnp.bfloat16)
    cell_order = jax.vmap(lambda own: jax.random.permutation(own, CELLS))(jax.random.split(splits[1], N_LAT * N_LON)).reshape((N_LAT, N_LON, CELLS)).astype(jnp.int32)
    map_weights = jnp.clip(0.001953125 * jax.random.uniform(splits[2], (N_LAT, N_LON, SRC, CB, R), jnp.float32) ** level_of(splits[2], (N_LAT, N_LON, SRC, CB, R), ((0, 8), (1, 16)), -0.2, 0.2), 0.0, 0.001953125).astype(jnp.bfloat16)
    dest_device_keys = jax.random.split(jax.random.fold_in(splits[3], 1), N_LAT * N_LON * SRC // SRC)
    dest_device_turns = jax.random.permutation(jax.random.fold_in(splits[3], 3), N_LAT * N_LON * SRC // SRC)
    dest_device = jax.vmap(lambda own, number: deal_out(jax.random.fold_in(splits[3], 2), own, number, SRC, N_LAT * N_LON, 1, SLOT, 0))(dest_device_keys, dest_device_turns).reshape((N_LAT, N_LON, SRC, 1))
    dest_block = plant(jax.random.randint(splits[4], (N_LAT, N_LON, SRC), 0, BLK), jax.random.fold_in(splits[4], 1), 0, BLK - 1).astype(jnp.int32)
    initial_flow = jnp.clip(0.2 + 0.8 * jax.random.uniform(splits[5], (N_LAT, N_LON, BLK, R), jnp.float32) ** level_of(splits[5], (N_LAT, N_LON, BLK, R), ((0, 8), (1, 16)), -0.2, 0.2), 0.2, 1.0)
    musk_k = draw_musk_k(jax.random.fold_in(splits[11], 71), 0)
    musk_x = draw_musk_x(jax.random.fold_in(splits[11], 71), 0)
    down_reach = draw_down_reach(jax.random.fold_in(splits[11], 71), 0)
    block_inverse = draw_block_inverse(jax.random.fold_in(splits[11], 71), 0)
    upstream_link = jax.vmap(lambda own: jax.random.permutation(own, BLK))(jax.random.split(splits[10], N_LAT * N_LON)).reshape((N_LAT, N_LON, BLK)).astype(jnp.int32)
    return {"runoff": runoff, "cell_order": cell_order, "map_weights": map_weights, "dest_device": dest_device, "dest_block": dest_block, "initial_flow": initial_flow, "musk_k": musk_k, "musk_x": musk_x, "down_reach": down_reach, "block_inverse": block_inverse, "upstream_link": upstream_link}


substep_seconds = 300.0


def coefficients(travel, weighting):
    half = 0.5 * substep_seconds
    denom = travel * (1.0 - weighting) + half
    first = (half - travel * weighting) / denom
    second = (half + travel * weighting) / denom
    third = (travel * (1.0 - weighting) - half) / denom
    return first, second, third


def device_terms(pieces):
    tile, order, weights = pieces
    picked = jnp.take(tile, order, axis=1).reshape(STEPS, SRC, CB).astype(jnp.float32)
    return jnp.einsum("tsc,scr->str", picked, weights.astype(jnp.float32), precision=lax.Precision.HIGHEST)


def reference(runoff, cell_order, map_weights, dest_device, dest_block, initial_flow, musk_k, musk_x, down_reach, block_inverse, upstream_link):
    devices = N_LAT * N_LON
    tiles = runoff.reshape(STEPS, N_LAT, CLAT, N_LON, CLON).transpose(1, 3, 0, 2, 4).reshape(devices, STEPS, CELLS)
    contrib = lax.map(device_terms, (tiles, cell_order.reshape(devices, CELLS), map_weights.reshape(devices, SRC, CB, R)))
    targets = (dest_device[..., 0] * BLK + dest_block).reshape(-1).astype(jnp.int32)
    lateral = jax.ops.segment_sum(contrib.reshape(devices * SRC, STEPS, R), targets, num_segments=devices * BLK)
    lateral = lateral.reshape(N_LAT, N_LON, BLK, STEPS, R)

    first, second, third = coefficients(musk_k, musk_x)
    block_ids = jnp.arange(devices * BLK, dtype=jnp.int32).reshape(N_LAT, N_LON, BLK, 1)
    segment_ids = (block_ids * (R + 1) + down_reach).reshape(-1).astype(jnp.int32)

    def upstream_sum(flow):
        total = jax.ops.segment_sum(flow.reshape(-1), segment_ids, num_segments=devices * BLK * (R + 1))
        return total.reshape(N_LAT, N_LON, BLK, R + 1)[..., :R]

    head_gain = first[..., 0:1] * block_inverse[..., :, 0]
    outlet_gain = head_gain[..., R - 1]

    def from_upstream(outlets):
        shifted = jnp.concatenate([jnp.zeros((N_LAT, 1, BLK), jnp.float32), outlets[:, :-1]], axis=1)
        return jnp.take_along_axis(shifted, upstream_link, axis=2)

    flow = initial_flow
    inflow_prev = from_upstream(initial_flow[..., R - 1])
    for step in range(STEPS):
        known = (first + second) * lateral[..., step, :] + second * upstream_sum(flow) + third * flow
        known = known.at[..., 0].add(second[..., 0] * inflow_prev)
        local = jnp.einsum("aobrs,aobs->aobr", block_inverse, known, precision=lax.Precision.HIGHEST)
        columns = [jnp.zeros((N_LAT, BLK), jnp.float32)]
        for column in range(1, N_LON):
            outlet = local[:, column - 1, :, R - 1] + outlet_gain[:, column - 1] * columns[column - 1]
            columns.append(jnp.take_along_axis(outlet, upstream_link[:, column], axis=1))
        inflow = jnp.stack(columns, axis=1)
        flow = local + head_gain * inflow[..., None]
        inflow_prev = inflow
    return flow
```

```python
import functools
import jax
import jax.numpy as jnp
from jax import lax
from jax.experimental import pallas as pl
from jax.experimental.pallas import tpu as pltpu
from jax.sharding import PartitionSpec as P

substep_seconds = 300.0

VREGS = 32
CHUNKS = 4

def gathered(x, index, axis):
    return jnp.take_along_axis(x, index, axis=axis, mode="promise_in_bounds")

def map_kernel(slots, order_ref, runoff_ref, target_ref, weights_ref, out_ref,
               pick_ref, held_ref, marks_ref, subs_ref, lanes_ref, counts_ref, sems):
    sources = weights_ref.shape[0]
    part = sources // CHUNKS
    def fetch(i):
        rows = pl.ds(i * part, part)
        return pltpu.make_async_copy(weights_ref.at[rows], held_ref.at[rows], sems.at[i])
    for i in range(CHUNKS):
        fetch(i).start()

    lane = lax.broadcasted_iota(jnp.int32, (8, 128), 1)
    sub = lax.broadcasted_iota(jnp.int32, (8, 128), 0)
    keys = []
    for v in range(VREGS):
        c = order_ref[pl.ds(8 * v, 8), :]
        keys.append(((c & 127) << 8) | (((c >> 8) & 7) << 5) | (((c >> 7) & 1) << 4) | (c >> 11))

    def flips(q):
        if q == 0 or q >= 15:
            return [None] * VREGS
        if q < 5:
            return [bool((v >> q) & 1) for v in range(VREGS)]
        bit = (sub >> (q - 5)) & 1 if q < 8 else (lane >> (q - 8)) & 1
        return [bit] * VREGS

    def as_word(flip):
        if flip is None or flip is False:
            return None
        if flip is True:
            return -1
        return -flip

    pair = 0
    undo = []
    for q in range(1, 16):
        before, now = flips(q - 1), flips(q)
        for v in range(VREGS):
            a, b = as_word(before[v]), as_word(now[v])
            if a is None and b is None:
                continue
            if isinstance(a, int) and isinstance(b, int):
                continue
            word = b if a is None else (a if b is None else a ^ b)
            keys[v] = keys[v] ^ word
        lane_bits = [k for k in range(q - 1, 7, -1)]
        sub_bits = [k for k in range(min(q - 1, 7), 4, -1)]
        for bits, axis, place, low, ref in ((lane_bits, 1, lane, 8, lanes_ref), (sub_bits, 0, sub, 5, subs_ref)):
            if not bits:
                continue
            marks = [[] for _ in range(VREGS)]
            for k in bits:
                d = 1 << (k - low)
                partner = place ^ d
                upper = (place & d) != 0
                for v in range(VREGS):
                    other = gathered(keys[v], partner, axis)
                    new = jnp.where(upper, jnp.maximum(keys[v], other), jnp.minimum(keys[v], other))
                    marks[v].append((new != keys[v], partner))
                    keys[v] = new
            row = (q - 9) if axis == 1 else (q - 6)
            for v in range(VREGS):
                index = place
                for mark, partner in reversed(marks[v]):
                    other = partner if index is place else gathered(index, partner, axis)
                    index = jnp.where(mark, other, index)
                ref[row * VREGS + v] = index
        pairs = []
        for k in range(min(q - 1, 4), -1, -1):
            for v in range(VREGS):
                if v & (1 << k):
                    continue
                w = v | (1 << k)
                a, b = keys[v], keys[w]
                marks_ref[pair] = (a > b).astype(jnp.int32)
                keys[v], keys[w] = jnp.minimum(a, b), jnp.maximum(a, b)
                pairs.append((pair, v, w))
                pair += 1
        undo.append((q, pairs))

    planes = runoff_ref.shape[0] // 2

    def plane(p, carry):
        low = (runoff_ref[p].astype(jnp.float32) * 4096.0).astype(jnp.int32)
        high = (runoff_ref[p + planes].astype(jnp.float32) * 4096.0).astype(jnp.int32)
        both = low | (high << 16)
        x = []
        for h in range(2):
            for r in range(16):
                x.append(both[8 * r:8 * r + 8, 128 * h:128 * h + 128])
        for q, pairs in reversed(undo):
            for at, v, w in reversed(pairs):
                mark = marks_ref[at] != 0
                x[v], x[w] = jnp.where(mark, x[w], x[v]), jnp.where(mark, x[v], x[w])
            if q >= 6:
                for v in range(VREGS):
                    x[v] = gathered(x[v], subs_ref[(q - 6) * VREGS + v], 0)
            if q >= 9:
                for v in range(VREGS):
                    x[v] = gathered(x[v], lanes_ref[(q - 9) * VREGS + v], 1)
        scale = 1.0 / 4096.0
        for v in range(VREGS):
            pick_ref[pl.ds(128 * v + p, 8, stride=16), :] = (x[v] & 0xFFFF).astype(jnp.float32) * scale
            pick_ref[pl.ds(128 * v + p + planes, 8, stride=16), :] = (x[v] >> 16).astype(jnp.float32) * scale
        return carry

    lax.fori_loop(0, planes, plane, 0)

    out_ref[...] = jnp.zeros_like(out_ref)
    def clear(d, carry):
        counts_ref[d] = 0
        return carry
    lax.fori_loop(0, counts_ref.shape[0], clear, 0)
    steps = 2 * planes
    unroll = 8
    for i in range(CHUNKS):
        fetch(i).wait()
        def group(g, carry):
            for u in range(unroll):
                s = i * part + g * unroll + u
                lhs = pick_ref[pl.ds(pl.multiple_of(s * 16, 16), 16), :].astype(jnp.bfloat16)
                c = jnp.dot(lhs, held_ref[s], preferred_element_type=jnp.float32)
                d = target_ref[s]
                k = counts_ref[d]
                counts_ref[d] = k + 1
                out_ref[pl.ds(d * (slots * steps) + k, steps, stride=slots), :] = c[:steps]
            return carry
        lax.fori_loop(0, part // unroll, group, 0)


def map_sources(order, runoff, target, weights, devices, slots):
    steps = runoff.shape[0]
    sources, cells, reaches = weights.shape
    vmem = pl.BlockSpec(memory_space=pltpu.VMEM)
    return pl.pallas_call(
        functools.partial(map_kernel, slots),
        out_shape=jax.ShapeDtypeStruct((devices * slots * steps, reaches), jnp.float32),
        in_specs=[vmem, vmem, pl.BlockSpec(memory_space=pltpu.SMEM), pl.BlockSpec(memory_space=pl.ANY)],
        out_specs=vmem,
        scratch_shapes=[
            pltpu.VMEM((sources * 16, cells), jnp.float32),
            pltpu.VMEM(weights.shape, weights.dtype),
            pltpu.VMEM((1040, 8, 128), jnp.int32),
            pltpu.VMEM((10 * VREGS, 8, 128), jnp.int32),
            pltpu.VMEM((7 * VREGS, 8, 128), jnp.int32),
            pltpu.SMEM((devices,), jnp.int32),
            pltpu.SemaphoreType.DMA((CHUNKS,)),
        ],
        compiler_params=pltpu.CompilerParams(vmem_limit_bytes=56 * 1024 * 1024),
    )(order, runoff, target, weights)


def coefficients(travel, weighting):
    half = 0.5 * substep_seconds
    denom = travel * (1.0 - weighting) + half
    first = (half - travel * weighting) / denom
    second = (half + travel * weighting) / denom
    third = (travel * (1.0 - weighting) - half) / denom
    return first, second, third


TILES = 16
SIZE = 128


def prepare_kernel(steps, slots, inverse_ref, travel_ref, weighting_ref, drains_ref, flow_ref, links_ref,
                   targets_ref, blocks_ref, me_ref, spread_ref, rows_ref, heads_ref, terms_ref, note_ref,
                   select_ref, left_ref, scaled_ref, product_ref):
    first, second, third = coefficients(travel_ref[...], weighting_ref[...])
    drains = drains_ref[...]
    nearest = jnp.minimum(drains, SIZE - 1)
    below = jnp.concatenate(
        [gathered(second[8 * i:8 * i + 8], nearest[8 * i:8 * i + 8], 1) for i in range(TILES)], axis=0)
    below = jnp.where(drains < SIZE, below, 0.0)
    ratio = below / first
    terms_ref[0] = (ratio + third).T
    terms_ref[1] = ratio.T
    terms_ref[2] = (first + second).T
    terms_ref[3] = flow_ref[...].T
    note_ref[...] = jnp.zeros_like(note_ref)
    note_ref[0:1, :] = terms_ref[3, SIZE - 1:SIZE, :]
    note_ref[13:14, :] = first.T[0:1, :]
    note_ref[14:15, :] = second.T[0:1, :]
    note_ref[15:16, :] = links_ref[...].astype(jnp.float32)

    hits = targets_ref[...] == me_ref[0]
    sources = hits.shape[1]
    order = lax.broadcasted_iota(jnp.int32, (sources, sources), 0)
    later = (order <= lax.broadcasted_iota(jnp.int32, (sources, sources), 1)).astype(jnp.bfloat16)
    place = jnp.dot(hits.astype(jnp.bfloat16), later, preferred_element_type=jnp.float32)
    column = lax.broadcasted_iota(jnp.int32, (SIZE, SIZE), 1).astype(jnp.float32)
    numbers = blocks_ref[...].astype(jnp.float32) + 1.0
    for k in range(slots):
        here = hits & (place == k + 1.0)
        named = jnp.sum(jnp.where(here, numbers, 0.0), axis=1, keepdims=True) - 1.0
        select_ref[k] = (named == column).astype(jnp.float32).T.astype(jnp.bfloat16)

    def turned(g, carry):
        for u in range(4):
            r = g * 4 + u
            spread_ref[pl.ds(r, SIZE, stride=SIZE), :] = inverse_ref[pl.ds(r, SIZE, stride=SIZE), :].T
        return carry

    lax.fori_loop(0, SIZE // 4, turned, 0)

    left_ref[...] = (lax.broadcasted_iota(jnp.int32, (SIZE, SIZE), 0) == SIZE - 1).astype(jnp.float32)
    heads_ref[0] = spread_ref[0:SIZE, :]

    def power(k, carry):
        head = heads_ref[k]
        scaled_ref[...] = terms_ref[0] * head
        left = [left_ref[8 * i:8 * i + 8, :] for i in range(TILES)]
        sums = [jnp.zeros((8, SIZE), jnp.float32) for _ in range(TILES)]
        for s in range(SIZE):
            factor = scaled_ref[s:s + 1, :]
            total = None
            for i in range(s // 8, TILES):
                part = spread_ref[s * SIZE + 8 * i:s * SIZE + 8 * i + 8, :]
                sums[i] = sums[i] + part * factor
                term = part * left[i]
                total = term if total is None else total + term
            product_ref[s:s + 1, :] = jnp.sum(total, axis=0, keepdims=True)
        after = jnp.minimum(k + 1, steps - 1)
        heads = jnp.concatenate(sums, axis=0) - terms_ref[1] * head
        @pl.when(k < steps - 1)
        def _():
            heads_ref[after] = heads
        product = product_ref[...]
        rows_ref[k] = product * terms_ref[2]
        note_ref[pl.ds(16 + k, 1), :] = product[0:1, :]
        new = product * terms_ref[0] - left_ref[...] * terms_ref[1]
        left_ref[...] = new
        note_ref[pl.ds(1 + k, 1), :] = jnp.sum(new * terms_ref[3], axis=0, keepdims=True)
        return carry

    lax.fori_loop(0, steps, power, 0)


def lateral_kernel(steps, slots, arrived_ref, select_ref, rows_ref, note_ref, lateral_ref, notes_ref):
    sources = arrived_ref.shape[0] // (slots * steps)
    for t in range(steps):
        total = None
        for k in range(slots):
            piece = arrived_ref[pl.ds(t * slots + k, sources, stride=slots * steps), :]
            high = piece.astype(jnp.bfloat16)
            low = (piece - high.astype(jnp.float32)).astype(jnp.bfloat16)
            for part in (high, low):
                term = jnp.dot(select_ref[k], part, preferred_element_type=jnp.float32)
                total = term if total is None else total + term
        lateral_ref[t] = total.T
    sums = [jnp.zeros((8, SIZE), jnp.float32) for _ in range(steps)]
    for i in range(TILES):
        tile = slice(8 * i, 8 * i + 8)
        given = [lateral_ref[t, tile, :] for t in range(steps)]
        weight = [rows_ref[t, tile, :] for t in range(steps)]
        for t in range(steps):
            for j in range(t + 1):
                sums[t] = sums[t] + weight[t - j] * given[j]
    note = note_ref[...]
    series = [jnp.sum(part, axis=0, keepdims=True) for part in sums]
    whole = jnp.concatenate(
        [note[0:1]] + [note[1 + t:2 + t] + series[t] for t in range(steps)] + [note[1 + steps:]], axis=0)
    for d in range(notes_ref.shape[0]):
        notes_ref[d] = whole


def local_kernel(steps, spread_ref, terms_ref, lateral_ref, flow_ref, scaled_ref, held_ref, sems):
    def fetch(i):
        rows = pl.ds(i * 2048, 2048)
        return pltpu.make_async_copy(spread_ref.at[rows], held_ref.at[rows], sems.at[i])

    for i in range(8):
        fetch(i).start()
    flow_ref[...] = terms_ref[3]

    def step(t, wait):
        flow = flow_ref[...]
        scaled_ref[...] = terms_ref[0] * flow + terms_ref[2] * lateral_ref[t]
        sums = [jnp.zeros((8, SIZE), jnp.float32) for _ in range(TILES)]
        for s in range(SIZE):
            if wait and s % 16 == 0:
                fetch(s // 16).wait()
            factor = scaled_ref[s:s + 1, :]
            for i in range(s // 8, TILES):
                sums[i] = sums[i] + held_ref[s * SIZE + 8 * i:s * SIZE + 8 * i + 8, :] * factor
        flow_ref[...] = jnp.concatenate(sums, axis=0) - terms_ref[1] * flow

    step(0, True)

    def rest(t, carry):
        step(t, False)
        return carry

    lax.fori_loop(1, steps, rest, 0)


def chain_kernel(steps, notes_ref, flow_ref, heads_ref, lon_ref, out_ref, pad_ref):
    count = notes_ref.shape[0]
    me = lon_ref[0]
    row = lax.broadcasted_iota(jnp.int32, (16, SIZE), 0)
    zeros = jnp.zeros((16, SIZE), jnp.float32)
    for k in range(count):
        pad_ref[k, 0:16, :] = zeros
        pad_ref[k, 16:32, :] = notes_ref[k, 16:32, :]

    def inlet(k, series):
        link = jnp.broadcast_to(notes_ref[k, 15:16, :].astype(jnp.int32), (16, SIZE))
        coming = jnp.concatenate([gathered(series[0:8], link[0:8], 1), gathered(series[8:16], link[0:8], 1)], axis=0)
        coming = jnp.where(row <= steps, coming, 0.0)
        return notes_ref[k, 13:14, :] * coming + notes_ref[k, 14:15, :] * pltpu.roll(coming, 1, 0)

    def hop(k, series):
        entering = inlet(k, series)
        new = notes_ref[k, 0:16, :]
        for t in range(1, steps + 1):
            new = new + pad_ref[k, 16 - t:32 - t, :] * entering[t:t + 1, :]
        return new

    series = lax.fori_loop(1, me, hop, notes_ref[0, 0:16, :])
    entering = jnp.where(me > 0, inlet(me, series), 0.0)
    flow = flow_ref[...]
    for t in range(1, steps + 1):
        flow = flow + heads_ref[steps - t] * entering[t:t + 1, :]
    out_ref[...] = flow.T


def body(runoff, cell_order, map_weights, dest_device, dest_block, initial_flow, musk_k, musk_x, down_reach,
         block_inverse, upstream_link):
    steps = runoff.shape[0]
    lat_count, lon_count = lax.axis_size("lat"), lax.axis_size("lon")
    devices = lat_count * lon_count
    lon_index = lax.axis_index("lon")
    my_index = lax.axis_index("lat") * lon_count + lon_index
    weights = map_weights.reshape(map_weights.shape[2:])
    sources, cells, reaches = weights.shape
    slots = 4
    targets = dest_device.reshape(devices, sources)
    my_targets = lax.dynamic_index_in_dim(targets, my_index, 0, keepdims=False)
    outgoing = map_sources(cell_order.reshape(sources, cells), runoff, my_targets, weights, devices, slots)
    arrived = lax.all_to_all(outgoing.reshape(devices, slots * steps, reaches), ("lat", "lon"),
                             split_axis=0, concat_axis=0, tiled=True)
    arrived = arrived.reshape(devices * slots * steps, reaches)

    vmem = pl.BlockSpec(memory_space=pltpu.VMEM)
    smem = pl.BlockSpec(memory_space=pltpu.SMEM)
    params = pltpu.CompilerParams(vmem_limit_bytes=56 * 1024 * 1024)
    blocks = initial_flow.shape[2]
    plane = (reaches, blocks)

    def made(*shape, dtype=jnp.float32):
        return jax.ShapeDtypeStruct(shape, dtype)

    spread, rows, heads, terms, note, select = pl.pallas_call(
        functools.partial(prepare_kernel, steps, slots),
        out_shape=[made(reaches * reaches, blocks), made(steps, *plane), made(steps, *plane), made(4, *plane),
                   made(32, blocks), made(slots, blocks, devices, dtype=jnp.bfloat16)],
        in_specs=[vmem] * 8 + [smem],
        out_specs=[vmem] * 6,
        scratch_shapes=[pltpu.VMEM(plane, jnp.float32)] * 3,
        compiler_params=params,
        cost_estimate=pl.CostEstimate(flops=2 * 24 * blocks * reaches * reaches, bytes_accessed=20 << 20, transcendentals=0),
    )(
        block_inverse.reshape(blocks * reaches, reaches),
        musk_k.reshape(blocks, reaches),
        musk_x.reshape(blocks, reaches),
        down_reach.reshape(blocks, reaches),
        initial_flow.reshape(blocks, reaches),
        upstream_link.reshape(1, blocks),
        targets,
        dest_block.reshape(devices, sources),
        my_index.reshape(1).astype(jnp.int32),
    )
    lateral, notes = pl.pallas_call(
        functools.partial(lateral_kernel, steps, slots),
        out_shape=[made(steps, *plane), made(lon_count, 32, blocks)],
        in_specs=[vmem] * 4,
        out_specs=[vmem] * 2,
        compiler_params=params,
    )(arrived, select, rows, note)
    notes = lax.all_to_all(notes, "lon", split_axis=0, concat_axis=0, tiled=True)
    flow = pl.pallas_call(
        functools.partial(local_kernel, steps),
        out_shape=made(*plane),
        in_specs=[pl.BlockSpec(memory_space=pl.ANY), vmem, vmem],
        out_specs=vmem,
        scratch_shapes=[pltpu.VMEM(plane, jnp.float32), pltpu.VMEM((reaches * reaches, blocks), jnp.float32),
                        pltpu.SemaphoreType.DMA((8,))],
        compiler_params=params,
        cost_estimate=pl.CostEstimate(flops=2 * 12 * blocks * reaches * reaches, bytes_accessed=10 << 20, transcendentals=0),
    )(spread, terms, lateral)
    result = pl.pallas_call(
        functools.partial(chain_kernel, steps),
        out_shape=made(blocks, reaches),
        in_specs=[vmem] * 3 + [smem],
        out_specs=vmem,
        scratch_shapes=[pltpu.VMEM((lon_count, 32, blocks), jnp.float32)],
        compiler_params=params,
    )(notes, flow, heads, lon_index.reshape(1).astype(jnp.int32))
    return result.reshape(initial_flow.shape)


def solution(mesh):
    return jax.shard_map(
        body,
        mesh=mesh,
        in_specs=(
            P(None, "lat", "lon"),
            P("lat", "lon", None),
            P("lat", "lon", None, None, None),
            P(),
            P(),
            P("lat", "lon", None, None),
            P("lat", "lon", None, None),
            P("lat", "lon", None, None),
            P("lat", "lon", None, None),
            P("lat", "lon", None, None, None),
            P("lat", "lon", None),
        ),
        out_specs=P("lat", "lon", None, None),
        check_vma=False,
    )
```

```python
import functools
import jax
import jax.numpy as jnp
from jax import lax
from jax.experimental import pallas as pl
from jax.experimental.pallas import tpu as pltpu
from jax.sharding import PartitionSpec as P

substep_seconds = 300.0

VREGS = 32
CHUNKS = 4
TOGETHER = 6

def gathered(x, index, axis):
    return jnp.take_along_axis(x, index, axis=axis, mode="promise_in_bounds")

def map_kernel(slots, far_order_ref, grid_ref, target_ref, weights_ref, out_ref,
               order_ref, runoff_ref, pick_ref, held_ref, marks_ref, subs_ref, lanes_ref, counts_ref, sems):
    sources = weights_ref.shape[0]
    part = sources // CHUNKS
    def fetch(i):
        rows = pl.ds(i * part, part)
        return pltpu.make_async_copy(weights_ref.at[rows], held_ref.at[rows], sems.at[i])
    order_copy = pltpu.make_async_copy(far_order_ref, order_ref, sems.at[CHUNKS + 1])
    order_copy.start()
    grid_copy = pltpu.make_async_copy(grid_ref, runoff_ref, sems.at[CHUNKS])
    grid_copy.start()
    for i in range(CHUNKS):
        fetch(i).start()

    out_ref[...] = jnp.zeros_like(out_ref)
    def clear(d, carry):
        counts_ref[d] = 0
        return carry
    lax.fori_loop(0, counts_ref.shape[0], clear, 0)
    order_copy.wait()

    lane = lax.broadcasted_iota(jnp.int32, (8, 128), 1)
    sub = lax.broadcasted_iota(jnp.int32, (8, 128), 0)
    keys = []
    for v in range(VREGS):
        c = order_ref[pl.ds(8 * v, 8), :]
        keys.append(((c & 127) << 8) | (((c >> 8) & 7) << 5) | (((c >> 7) & 1) << 4) | (c >> 11))

    def flips(q):
        if q == 0 or q >= 15:
            return [None] * VREGS
        if q < 5:
            return [bool((v >> q) & 1) for v in range(VREGS)]
        bit = (sub >> (q - 5)) & 1 if q < 8 else (lane >> (q - 8)) & 1
        return [bit] * VREGS

    def as_word(flip):
        if flip is None or flip is False:
            return None
        if flip is True:
            return -1
        return -flip

    pair = 0
    undo = []
    for q in range(1, 16):
        before, now = flips(q - 1), flips(q)
        for v in range(VREGS):
            a, b = as_word(before[v]), as_word(now[v])
            if a is None and b is None:
                continue
            if isinstance(a, int) and isinstance(b, int):
                continue
            word = b if a is None else (a if b is None else a ^ b)
            keys[v] = keys[v] ^ word
        lane_bits = [k for k in range(q - 1, 7, -1)]
        sub_bits = [k for k in range(min(q - 1, 7), 4, -1)]
        for bits, axis, place, low, ref in ((lane_bits, 1, lane, 8, lanes_ref), (sub_bits, 0, sub, 5, subs_ref)):
            if not bits:
                continue
            marks = [[] for _ in range(VREGS)]
            for k in bits:
                d = 1 << (k - low)
                partner = place ^ d
                upper = (place & d) != 0
                for v in range(VREGS):
                    other = gathered(keys[v], partner, axis)
                    new = jnp.where(upper, jnp.maximum(keys[v], other), jnp.minimum(keys[v], other))
                    marks[v].append((new != keys[v], partner))
                    keys[v] = new
            row = (q - 9) if axis == 1 else (q - 6)
            for v in range(VREGS):
                index = place
                for mark, partner in reversed(marks[v]):
                    other = partner if index is place else gathered(index, partner, axis)
                    index = jnp.where(mark, other, index)
                ref[row * VREGS + v] = index
        pairs = []
        for k in range(min(q - 1, 4), -1, -1):
            for v in range(VREGS):
                if v & (1 << k):
                    continue
                w = v | (1 << k)
                a, b = keys[v], keys[w]
                marks_ref[pair] = (a > b).astype(jnp.int32)
                keys[v], keys[w] = jnp.minimum(a, b), jnp.maximum(a, b)
                pairs.append((pair, v, w))
                pair += 1
        undo.append((q, pairs))

    planes = runoff_ref.shape[0] // 2
    grid_copy.wait()

    def several(g, carry):
        first = g * TOGETHER
        xs = []
        for n in range(TOGETHER):
            p = first + n
            low = (runoff_ref[p].astype(jnp.float32) * 4096.0).astype(jnp.int32)
            high = (runoff_ref[p + planes].astype(jnp.float32) * 4096.0).astype(jnp.int32)
            both = low | (high << 16)
            xs.append([both[8 * r:8 * r + 8, 128 * h:128 * h + 128] for h in range(2) for r in range(16)])
        for q, pairs in reversed(undo):
            for x in xs:
                for at, v, w in reversed(pairs):
                    mark = marks_ref[at] != 0
                    x[v], x[w] = jnp.where(mark, x[w], x[v]), jnp.where(mark, x[v], x[w])
                for v in range(VREGS):
                    if q >= 6:
                        x[v] = gathered(x[v], subs_ref[(q - 6) * VREGS + v], 0)
                    if q >= 9:
                        x[v] = gathered(x[v], lanes_ref[(q - 9) * VREGS + v], 1)
        scale = 1.0 / 4096.0
        for n, x in enumerate(xs):
            for v in range(VREGS):
                p = 128 * v + first + n
                pick_ref[pl.ds(p, 8, stride=16), :] = (x[v] & 0xFFFF).astype(jnp.float32) * scale
                pick_ref[pl.ds(p + planes, 8, stride=16), :] = (x[v] >> 16).astype(jnp.float32) * scale
        return carry

    lax.fori_loop(0, planes // TOGETHER, several, 0)

    steps = 2 * planes
    unroll = 64
    for i in range(CHUNKS):
        fetch(i).wait()
        def group(g, carry):
            for u in range(unroll):
                s = i * part + g * unroll + u
                lhs = pick_ref[pl.ds(pl.multiple_of(s * 16, 16), 16), :].astype(jnp.bfloat16)
                c = jnp.dot(lhs, held_ref[s], preferred_element_type=jnp.float32)
                d = target_ref[s]
                k = counts_ref[d]
                counts_ref[d] = k + 1
                out_ref[pl.ds(d * (slots * steps) + k, steps, stride=slots), :] = c[:steps]
            return carry
        lax.fori_loop(0, part // unroll, group, 0)


def map_sources(order, runoff, target, weights, devices, slots):
    steps = runoff.shape[0]
    sources, cells, reaches = weights.shape
    vmem = pl.BlockSpec(memory_space=pltpu.VMEM)
    far = pl.BlockSpec(memory_space=pltpu.HBM)
    return pl.pallas_call(
        functools.partial(map_kernel, slots),
        out_shape=jax.ShapeDtypeStruct((devices * slots * steps, reaches), jnp.float32),
        in_specs=[far, far, pl.BlockSpec(memory_space=pltpu.SMEM), far],
        out_specs=vmem,
        scratch_shapes=[
            pltpu.VMEM(order.shape, order.dtype),
            pltpu.VMEM(runoff.shape, runoff.dtype),
            pltpu.VMEM((sources * 16, cells), jnp.float32),
            pltpu.VMEM(weights.shape, weights.dtype),
            pltpu.VMEM((1040, 8, 128), jnp.int32),
            pltpu.VMEM((10 * VREGS, 8, 128), jnp.int32),
            pltpu.VMEM((7 * VREGS, 8, 128), jnp.int32),
            pltpu.SMEM((devices,), jnp.int32),
            pltpu.SemaphoreType.DMA((CHUNKS + 2,)),
        ],
        compiler_params=pltpu.CompilerParams(vmem_limit_bytes=52 << 20),
    )(pltpu.with_memory_space_constraint(order, pltpu.HBM), pltpu.with_memory_space_constraint(runoff, pltpu.HBM), target,
      pltpu.with_memory_space_constraint(weights, pltpu.HBM))


def coefficients(travel, weighting):
    half = 0.5 * substep_seconds
    denom = travel * (1.0 - weighting) + half
    first = (half - travel * weighting) / denom
    second = (half + travel * weighting) / denom
    third = (travel * (1.0 - weighting) - half) / denom
    return first, second, third


TILES = 16
SIZE = 128


def prepare_kernel(steps, slots, inverse_ref, travel_ref, weighting_ref, drains_ref, flow_ref, links_ref,
                   targets_ref, blocks_ref, me_ref, spread_ref, rows_ref, heads_ref, terms_ref, far_note_ref,
                   note_ref, left_ref, scaled_ref, product_ref, sem):
    first, second, third = coefficients(travel_ref[...], weighting_ref[...])
    drains = drains_ref[...]
    nearest = jnp.minimum(drains, SIZE - 1)
    below = jnp.concatenate(
        [gathered(second[8 * i:8 * i + 8], nearest[8 * i:8 * i + 8], 1) for i in range(TILES)], axis=0)
    below = jnp.where(drains < SIZE, below, 0.0)
    ratio = below / first
    terms_ref[0] = (ratio + third).T
    terms_ref[1] = ratio.T
    terms_ref[2] = (first + second).T
    terms_ref[3] = flow_ref[...].T
    note_ref[...] = jnp.zeros_like(note_ref)
    note_ref[0:1, :] = terms_ref[3, SIZE - 1:SIZE, :]
    note_ref[13:14, :] = first.T[0:1, :]
    note_ref[14:15, :] = second.T[0:1, :]
    note_ref[15:16, :] = links_ref[...].astype(jnp.float32)

    hits = targets_ref[...] == me_ref[0]
    sources = hits.shape[1]
    order = lax.broadcasted_iota(jnp.int32, (sources, sources), 0)
    later = (order <= lax.broadcasted_iota(jnp.int32, (sources, sources), 1)).astype(jnp.bfloat16)
    place = jnp.dot(hits.astype(jnp.bfloat16), later, preferred_element_type=jnp.float32)
    numbers = blocks_ref[...].astype(jnp.float32) + 1.0
    for k in range(slots):
        here = hits & (place == k + 1.0)
        named = jnp.sum(jnp.where(here, numbers, 0.0), axis=1, keepdims=True) - 1.0
        note_ref[32 + k:33 + k, :] = jnp.broadcast_to(named, (SIZE, SIZE)).T[0:1, :]

    def turned(g, carry):
        for u in range(4):
            r = g * 4 + u
            spread_ref[pl.ds(r, SIZE, stride=SIZE), :] = inverse_ref[pl.ds(r, SIZE, stride=SIZE), :].T
        return carry

    lax.fori_loop(0, SIZE // 4, turned, 0)

    left_ref[...] = (lax.broadcasted_iota(jnp.int32, (SIZE, SIZE), 0) == SIZE - 1).astype(jnp.float32)
    heads_ref[0] = spread_ref[0:SIZE, :]

    def power(k, carry):
        head = heads_ref[k]
        scaled_ref[...] = terms_ref[0] * head
        left = [left_ref[8 * i:8 * i + 8, :] for i in range(TILES)]
        sums = [jnp.zeros((8, SIZE), jnp.float32) for _ in range(TILES)]
        for s in range(SIZE):
            factor = scaled_ref[s:s + 1, :]
            total = None
            for i in range(s // 8, TILES):
                part = spread_ref[s * SIZE + 8 * i:s * SIZE + 8 * i + 8, :]
                sums[i] = sums[i] + part * factor
                term = part * left[i]
                total = term if total is None else total + term
            product_ref[s:s + 1, :] = jnp.sum(total, axis=0, keepdims=True)
        after = jnp.minimum(k + 1, steps - 1)
        heads = jnp.concatenate(sums, axis=0) - terms_ref[1] * head
        @pl.when(k < steps - 1)
        def _():
            heads_ref[after] = heads
        product = product_ref[...]
        rows_ref[k] = product * terms_ref[2]
        note_ref[pl.ds(16 + k, 1), :] = product[0:1, :]
        new = product * terms_ref[0] - left_ref[...] * terms_ref[1]
        left_ref[...] = new
        note_ref[pl.ds(1 + k, 1), :] = jnp.sum(new * terms_ref[3], axis=0, keepdims=True)
        return carry

    lax.fori_loop(0, steps, power, 0)
    store = pltpu.make_async_copy(note_ref, far_note_ref, sem)
    store.start()
    store.wait()


def lateral_kernel(steps, slots, arrived_ref, far_note_ref, far_rows_ref, far_lateral_ref, far_notes_ref,
                   note_ref, rows_ref, lateral_ref, notes_ref, sems):
    opening = pltpu.make_async_copy(far_note_ref, note_ref, sems.at[2])
    opening.start()
    fetch = pltpu.make_async_copy(far_rows_ref, rows_ref, sems.at[0])
    fetch.start()
    sources = arrived_ref.shape[0] // (slots * steps)
    opening.wait()
    block = lax.broadcasted_iota(jnp.int32, (SIZE, sources), 0).astype(jnp.float32)
    select = [(note_ref[32 + k:33 + k, :] == block).astype(jnp.bfloat16) for k in range(slots)]
    for t in range(steps):
        total = None
        for k in range(slots):
            piece = arrived_ref[pl.ds(t * slots + k, sources, stride=slots * steps), :]
            high = piece.astype(jnp.bfloat16)
            low = (piece - high.astype(jnp.float32)).astype(jnp.bfloat16)
            for part in (high, low):
                term = jnp.dot(select[k], part, preferred_element_type=jnp.float32)
                total = term if total is None else total + term
        lateral_ref[t] = total.T
    store = pltpu.make_async_copy(lateral_ref, far_lateral_ref, sems.at[1])
    store.start()
    fetch.wait()
    sums = [jnp.zeros((8, SIZE), jnp.float32) for _ in range(steps)]
    for i in range(TILES):
        tile = slice(8 * i, 8 * i + 8)
        given = [lateral_ref[t, tile, :] for t in range(steps)]
        weight = [rows_ref[t, tile, :] for t in range(steps)]
        for t in range(steps):
            for j in range(t + 1):
                sums[t] = sums[t] + weight[t - j] * given[j]
    note = note_ref[0:32, :]
    series = [jnp.sum(part, axis=0, keepdims=True) for part in sums]
    whole = jnp.concatenate(
        [note[0:1]] + [note[1 + t:2 + t] + series[t] for t in range(steps)] + [note[1 + steps:]], axis=0)
    for d in range(notes_ref.shape[0]):
        notes_ref[d] = whole
    send = pltpu.make_async_copy(notes_ref, far_notes_ref, sems.at[3])
    send.start()
    send.wait()
    store.wait()


def local_kernel(steps, terms_ref, far_spread_ref, far_lateral_ref, flow_ref, spread_ref, lateral_ref, scaled_ref, sems):
    def fetch(j):
        where = (pl.ds(8 * j, 8), pl.ds(8 * j, SIZE - 8 * j))
        return pltpu.make_async_copy(far_spread_ref.at[where], spread_ref.at[where], sems.at[j])

    given = pltpu.make_async_copy(far_lateral_ref, lateral_ref, sems.at[TILES])
    given.start()
    for j in range(TILES):
        fetch(j).start()
    flow_ref[...] = terms_ref[3]
    given.wait()

    def step(t, first):
        flow = flow_ref[...]
        scaled_ref[...] = terms_ref[0] * flow + terms_ref[2] * lateral_ref[t]
        sums = [jnp.zeros((8, SIZE), jnp.float32) for _ in range(TILES)]
        for s in range(SIZE):
            if first and s % 8 == 0:
                fetch(s // 8).wait()
            factor = scaled_ref[s:s + 1, :]
            for i in range(s // 8, TILES):
                sums[i] = sums[i] + spread_ref[s, 8 * i:8 * i + 8, :] * factor
        flow_ref[...] = jnp.concatenate(sums, axis=0) - terms_ref[1] * flow

    step(0, True)

    def rest(t, carry):
        step(t, False)
        return carry

    lax.fori_loop(1, steps, rest, 0)


def chain_kernel(steps, notes_ref, flow_ref, far_heads_ref, lon_ref, out_ref, pad_ref, heads_ref, sem):
    fetch = pltpu.make_async_copy(far_heads_ref, heads_ref, sem)
    fetch.start()
    count = notes_ref.shape[0]
    me = lon_ref[0]
    row = lax.broadcasted_iota(jnp.int32, (16, SIZE), 0)
    zeros = jnp.zeros((16, SIZE), jnp.float32)
    for k in range(count):
        pad_ref[k, 0:16, :] = zeros
        pad_ref[k, 16:32, :] = notes_ref[k, 16:32, :]

    def inlet(k, series):
        link = jnp.broadcast_to(notes_ref[k, 15:16, :].astype(jnp.int32), (16, SIZE))
        coming = jnp.concatenate([gathered(series[0:8], link[0:8], 1), gathered(series[8:16], link[0:8], 1)], axis=0)
        coming = jnp.where(row <= steps, coming, 0.0)
        return notes_ref[k, 13:14, :] * coming + notes_ref[k, 14:15, :] * pltpu.roll(coming, 1, 0)

    def hop(k, series):
        entering = inlet(k, series)
        new = notes_ref[k, 0:16, :]
        for t in range(1, steps + 1):
            new = new + pad_ref[k, 16 - t:32 - t, :] * entering[t:t + 1, :]
        return new

    series = lax.fori_loop(1, me, hop, notes_ref[0, 0:16, :])
    entering = jnp.where(me > 0, inlet(me, series), 0.0)
    fetch.wait()
    flow = flow_ref[...]
    for t in range(1, steps + 1):
        flow = flow + heads_ref[steps - t] * entering[t:t + 1, :]
    out_ref[...] = flow.T


def body(runoff, cell_order, map_weights, dest_device, dest_block, initial_flow, musk_k, musk_x, down_reach,
         block_inverse, upstream_link):
    steps = runoff.shape[0]
    lat_count, lon_count = lax.axis_size("lat"), lax.axis_size("lon")
    devices = lat_count * lon_count
    lon_index = lax.axis_index("lon")
    my_index = lax.axis_index("lat") * lon_count + lon_index
    weights = map_weights.reshape(map_weights.shape[2:])
    sources, cells, reaches = weights.shape
    slots = 4
    targets = dest_device.reshape(devices, sources)
    my_targets = lax.dynamic_slice(dest_device, (lax.axis_index("lat"), lon_index, 0, 0), (1, 1, sources, 1))
    my_targets = my_targets.reshape(sources)
    outgoing = map_sources(cell_order.reshape(sources, cells), runoff, my_targets, weights, devices, slots)
    arrived = lax.all_to_all(outgoing.reshape(devices, slots * steps, reaches), ("lat", "lon"),
                             split_axis=0, concat_axis=0, tiled=True)
    arrived = arrived.reshape(devices * slots * steps, reaches)

    vmem = pl.BlockSpec(memory_space=pltpu.VMEM)
    smem = pl.BlockSpec(memory_space=pltpu.SMEM)

    def params(mib):
        return pltpu.CompilerParams(vmem_limit_bytes=mib << 20)

    def near(x):
        return pltpu.with_memory_space_constraint(x, pltpu.VMEM)

    def away(x):
        return pltpu.with_memory_space_constraint(x, pltpu.HBM)

    far = pl.BlockSpec(memory_space=pltpu.HBM)
    blocks = initial_flow.shape[2]
    plane = (reaches, blocks)
    moves = pltpu.SemaphoreType.DMA

    def made(*shape):
        return jax.ShapeDtypeStruct(shape, jnp.float32)

    spread, rows, heads, terms, note = pl.pallas_call(
        functools.partial(prepare_kernel, steps, slots),
        out_shape=[made(reaches * reaches, blocks), made(steps, *plane), made(steps, *plane), made(4, *plane),
                   pltpu.HBM((40, blocks), jnp.float32)],
        in_specs=[vmem] * 8 + [smem],
        out_specs=[vmem] * 4 + [far],
        scratch_shapes=[pltpu.VMEM((40, blocks), jnp.float32)] + [pltpu.VMEM(plane, jnp.float32)] * 3 + [moves],
        compiler_params=params(52),
        cost_estimate=pl.CostEstimate(flops=2 * 24 * blocks * reaches * reaches, bytes_accessed=20 << 20, transcendentals=0),
    )(
        block_inverse.reshape(blocks * reaches, reaches),
        musk_k.reshape(blocks, reaches),
        musk_x.reshape(blocks, reaches),
        down_reach.reshape(blocks, reaches),
        initial_flow.reshape(blocks, reaches),
        upstream_link.reshape(1, blocks),
        targets,
        dest_block.reshape(devices, sources),
        my_index.reshape(1).astype(jnp.int32),
    )
    lateral, notes = pl.pallas_call(
        functools.partial(lateral_kernel, steps, slots),
        out_shape=[pltpu.HBM((steps, *plane), jnp.float32), pltpu.HBM((lon_count, 32, blocks), jnp.float32)],
        in_specs=[vmem, far, far],
        out_specs=[far, far],
        scratch_shapes=[pltpu.VMEM((40, blocks), jnp.float32)] + [pltpu.VMEM((steps, *plane), jnp.float32)] * 2
        + [pltpu.VMEM((lon_count, 32, blocks), jnp.float32), moves((4,))],
        compiler_params=params(10),
    )(near(arrived), away(note), away(rows))
    notes = lax.all_to_all(notes, "lon", split_axis=0, concat_axis=0, tiled=True)
    flow = pl.pallas_call(
        functools.partial(local_kernel, steps),
        out_shape=made(*plane),
        in_specs=[vmem, far, far],
        out_specs=vmem,
        scratch_shapes=[pltpu.VMEM((reaches, *plane), jnp.float32), pltpu.VMEM((steps, *plane), jnp.float32),
                        pltpu.VMEM(plane, jnp.float32), moves((TILES + 1,))],
        compiler_params=params(52),
        cost_estimate=pl.CostEstimate(flops=2 * 12 * blocks * reaches * reaches, bytes_accessed=8 << 20, transcendentals=0),
    )(terms, away(spread.reshape(reaches, *plane)), away(lateral))
    result = pl.pallas_call(
        functools.partial(chain_kernel, steps),
        out_shape=made(blocks, reaches),
        in_specs=[vmem, vmem, far, smem],
        out_specs=vmem,
        scratch_shapes=[pltpu.VMEM((lon_count, 32, blocks), jnp.float32), pltpu.VMEM((steps, *plane), jnp.float32), moves],
        compiler_params=params(10),
    )(near(notes), flow, away(heads), lon_index.reshape(1).astype(jnp.int32))
    return result.reshape(initial_flow.shape)


def solution(mesh):
    return jax.shard_map(
        body,
        mesh=mesh,
        in_specs=(
            P(None, "lat", "lon"),
            P("lat", "lon", None),
            P("lat", "lon", None, None, None),
            P(),
            P(),
            P("lat", "lon", None, None),
            P("lat", "lon", None, None),
            P("lat", "lon", None, None),
            P("lat", "lon", None, None),
            P("lat", "lon", None, None, None),
            P("lat", "lon", None),
        ),
        out_specs=P("lat", "lon", None, None),
        check_vma=False,
    )
```

```python
import functools
import jax
import jax.numpy as jnp
from jax import lax
from jax.experimental import pallas as pl
from jax.experimental.pallas import tpu as pltpu
from jax.sharding import PartitionSpec as P

substep_seconds = 300.0

VREGS = 32
CHUNKS = 4
TOGETHER = 6

def gathered(x, index, axis):
    return jnp.take_along_axis(x, index, axis=axis, mode="promise_in_bounds")

def map_kernel(slots, far_order_ref, grid_ref, owners_ref, me_ref, weights_ref, out_ref,
               target_ref, order_ref, runoff_ref, pick_ref, held_ref, marks_ref, subs_ref, lanes_ref, counts_ref, sems):
    sources = weights_ref.shape[0]
    part = sources // CHUNKS
    def fetch(i):
        rows = pl.ds(i * part, part)
        return pltpu.make_async_copy(weights_ref.at[rows], held_ref.at[rows], sems.at[i])
    order_copy = pltpu.make_async_copy(far_order_ref, order_ref, sems.at[CHUNKS + 1])
    order_copy.start()
    per_device = weights_ref.shape[0] // 128
    first_row = me_ref[0] * per_device
    aligned = (first_row >> 3) << 3
    within = first_row - aligned
    target_copy = pltpu.make_async_copy(
        owners_ref.at[pl.ds(pl.multiple_of(aligned, 8), 8)], target_ref, sems.at[CHUNKS + 2])
    target_copy.start()
    grid_copy = pltpu.make_async_copy(grid_ref, runoff_ref, sems.at[CHUNKS])
    grid_copy.start()
    for i in range(CHUNKS):
        fetch(i).start()

    out_ref[...] = jnp.zeros_like(out_ref)
    def clear(d, carry):
        counts_ref[d] = 0
        return carry
    lax.fori_loop(0, counts_ref.shape[0], clear, 0)
    order_copy.wait()

    lane = lax.broadcasted_iota(jnp.int32, (8, 128), 1)
    sub = lax.broadcasted_iota(jnp.int32, (8, 128), 0)
    keys = []
    for v in range(VREGS):
        c = order_ref[pl.ds(8 * v, 8), :]
        keys.append(((c & 127) << 8) | (((c >> 8) & 7) << 5) | (((c >> 7) & 1) << 4) | (c >> 11))

    def flips(q):
        if q == 0 or q >= 15:
            return [None] * VREGS
        if q < 5:
            return [bool((v >> q) & 1) for v in range(VREGS)]
        bit = (sub >> (q - 5)) & 1 if q < 8 else (lane >> (q - 8)) & 1
        return [bit] * VREGS

    def as_word(flip):
        if flip is None or flip is False:
            return None
        if flip is True:
            return -1
        return -flip

    pair = 0
    undo = []
    for q in range(1, 16):
        before, now = flips(q - 1), flips(q)
        for v in range(VREGS):
            a, b = as_word(before[v]), as_word(now[v])
            if a is None and b is None:
                continue
            if isinstance(a, int) and isinstance(b, int):
                continue
            word = b if a is None else (a if b is None else a ^ b)
            keys[v] = keys[v] ^ word
        lane_bits = [k for k in range(q - 1, 7, -1)]
        sub_bits = [k for k in range(min(q - 1, 7), 4, -1)]
        for bits, axis, place, low, ref in ((lane_bits, 1, lane, 8, lanes_ref), (sub_bits, 0, sub, 5, subs_ref)):
            if not bits:
                continue
            marks = [[] for _ in range(VREGS)]
            for k in bits:
                d = 1 << (k - low)
                partner = place ^ d
                upper = (place & d) != 0
                for v in range(VREGS):
                    other = gathered(keys[v], partner, axis)
                    new = jnp.where(upper, jnp.maximum(keys[v], other), jnp.minimum(keys[v], other))
                    marks[v].append((new != keys[v], partner))
                    keys[v] = new
            row = (q - 9) if axis == 1 else (q - 6)
            index = [place] * VREGS
            for n in reversed(range(len(bits))):
                for v in range(VREGS):
                    mark, partner = marks[v][n]
                    other = partner if index[v] is place else gathered(index[v], partner, axis)
                    index[v] = jnp.where(mark, other, index[v])
            for v in range(VREGS):
                ref[row * VREGS + v] = index[v]
        pairs = []
        for k in range(min(q - 1, 4), -1, -1):
            for v in range(VREGS):
                if v & (1 << k):
                    continue
                w = v | (1 << k)
                a, b = keys[v], keys[w]
                marks_ref[pair] = (a > b).astype(jnp.int32)
                keys[v], keys[w] = jnp.minimum(a, b), jnp.maximum(a, b)
                pairs.append((pair, v, w))
                pair += 1
        undo.append((q, pairs))

    planes = runoff_ref.shape[0] // 2
    grid_copy.wait()

    def several(g, carry):
        first = g * TOGETHER
        xs = []
        for n in range(TOGETHER):
            p = first + n
            low = (runoff_ref[p].astype(jnp.float32) * 4096.0).astype(jnp.int32)
            high = (runoff_ref[p + planes].astype(jnp.float32) * 4096.0).astype(jnp.int32)
            both = low | (high << 16)
            xs.append([both[8 * r:8 * r + 8, 128 * h:128 * h + 128] for h in range(2) for r in range(16)])
        for q, pairs in reversed(undo):
            for base in range(0, TOGETHER, 2):
                some = xs[base:base + 2]
                for at, v, w in reversed(pairs):
                    mark = marks_ref[at] != 0
                    for x in some:
                        x[v], x[w] = jnp.where(mark, x[w], x[v]), jnp.where(mark, x[v], x[w])
                for v in range(VREGS):
                    if q >= 6:
                        index = subs_ref[(q - 6) * VREGS + v]
                        for x in some:
                            x[v] = gathered(x[v], index, 0)
            if q >= 9:
                for v in range(VREGS):
                    index = lanes_ref[(q - 9) * VREGS + v]
                    for x in xs:
                        x[v] = gathered(x[v], index, 1)
        scale = 1.0 / 4096.0
        for n, x in enumerate(xs):
            for v in range(VREGS):
                p = 128 * v + first + n
                pick_ref[pl.ds(p, 8, stride=16), :] = (x[v] & 0xFFFF).astype(jnp.float32) * scale
                pick_ref[pl.ds(p + planes, 8, stride=16), :] = (x[v] >> 16).astype(jnp.float32) * scale
        return carry

    lax.fori_loop(0, planes // TOGETHER, several, 0)

    target_copy.wait()
    steps = 2 * planes
    unroll = 64
    for i in range(CHUNKS):
        fetch(i).wait()
        def group(g, carry):
            for u in range(0, unroll, 2):
                s = i * part + g * unroll + u
                rows = pick_ref[pl.ds(pl.multiple_of(s * 16, 32), 32), :].astype(jnp.bfloat16)
                none = jnp.zeros((16, 128), jnp.bfloat16)
                lhs = jnp.concatenate([jnp.concatenate([rows[:16], none], 1), jnp.concatenate([none, rows[16:]], 1)], 0)
                both = jnp.dot(lhs, held_ref[pl.ds(s, 2)].reshape(256, 128), preferred_element_type=jnp.float32)
                for n in range(2):
                    d = target_ref[within + ((s + n) >> 7), (s + n) & 127]
                    k = counts_ref[d]
                    counts_ref[d] = k + 1
                    out_ref[pl.ds(d * (slots * steps) + k, steps, stride=slots), :] = both[16 * n:16 * n + steps]
            return carry
        lax.fori_loop(0, part // unroll, group, 0)


def away(x):
    return pltpu.with_memory_space_constraint(x, pltpu.HBM)


def map_sources(order, runoff, owners, me, weights, devices, slots):
    steps = runoff.shape[0]
    sources, cells, reaches = weights.shape
    vmem = pl.BlockSpec(memory_space=pltpu.VMEM)
    far = pl.BlockSpec(memory_space=pltpu.HBM)
    return pl.pallas_call(
        functools.partial(map_kernel, slots),
        out_shape=jax.ShapeDtypeStruct((devices * slots * steps, reaches), jnp.float32),
        in_specs=[far, far, far, pl.BlockSpec(memory_space=pltpu.SMEM), far],
        out_specs=vmem,
        scratch_shapes=[
            pltpu.SMEM((8, 128), jnp.int32),
            pltpu.VMEM(order.shape, order.dtype),
            pltpu.VMEM(runoff.shape, runoff.dtype),
            pltpu.VMEM((sources * 16, cells), jnp.float32),
            pltpu.VMEM(weights.shape, weights.dtype),
            pltpu.VMEM((1040, 8, 128), jnp.int32),
            pltpu.VMEM((10 * VREGS, 8, 128), jnp.int32),
            pltpu.VMEM((7 * VREGS, 8, 128), jnp.int32),
            pltpu.SMEM((devices,), jnp.int32),
            pltpu.SemaphoreType.DMA((CHUNKS + 3,)),
        ],
        compiler_params=pltpu.CompilerParams(vmem_limit_bytes=52 << 20),
    )(away(order), away(runoff), away(owners), me, away(weights))


def coefficients(travel, weighting):
    half = 0.5 * substep_seconds
    denom = travel * (1.0 - weighting) + half
    first = (half - travel * weighting) / denom
    second = (half + travel * weighting) / denom
    third = (travel * (1.0 - weighting) - half) / denom
    return first, second, third


TILES = 16
SIZE = 128


def prepare_kernel(steps, slots, inverse_ref, travel_ref, weighting_ref, drains_ref, flow_ref, links_ref,
                   targets_ref, blocks_ref, me_ref, spread_ref, rows_ref, heads_ref, terms_ref, far_note_ref,
                   note_ref, left_ref, scaled_ref, product_ref, sem):
    first, second, third = coefficients(travel_ref[...], weighting_ref[...])
    drains = drains_ref[...]
    nearest = jnp.minimum(drains, SIZE - 1)
    below = jnp.concatenate(
        [gathered(second[8 * i:8 * i + 8], nearest[8 * i:8 * i + 8], 1) for i in range(TILES)], axis=0)
    below = jnp.where(drains < SIZE, below, 0.0)
    ratio = below / first
    terms_ref[0] = (ratio + third).T
    terms_ref[1] = ratio.T
    terms_ref[2] = (first + second).T
    terms_ref[3] = flow_ref[...].T
    note_ref[...] = jnp.zeros_like(note_ref)
    note_ref[0:1, :] = terms_ref[3, SIZE - 1:SIZE, :]
    note_ref[13:14, :] = first.T[0:1, :]
    note_ref[14:15, :] = second.T[0:1, :]
    note_ref[15:16, :] = links_ref[...].astype(jnp.float32)

    hits = targets_ref[...] == me_ref[0]
    sources = hits.shape[1]
    order = lax.broadcasted_iota(jnp.int32, (sources, sources), 0)
    later = (order <= lax.broadcasted_iota(jnp.int32, (sources, sources), 1)).astype(jnp.bfloat16)
    place = jnp.dot(hits.astype(jnp.bfloat16), later, preferred_element_type=jnp.float32)
    numbers = blocks_ref[...].astype(jnp.float32) + 1.0
    for k in range(slots):
        here = hits & (place == k + 1.0)
        named = jnp.sum(jnp.where(here, numbers, 0.0), axis=1, keepdims=True) - 1.0
        note_ref[32 + k:33 + k, :] = jnp.broadcast_to(named, (SIZE, SIZE)).T[0:1, :]

    def turned(g, carry):
        for u in range(4):
            r = g * 4 + u
            spread_ref[pl.ds(r, SIZE, stride=SIZE), :] = inverse_ref[pl.ds(r, SIZE, stride=SIZE), :].T
        return carry

    lax.fori_loop(0, SIZE // 4, turned, 0)

    left_ref[...] = (lax.broadcasted_iota(jnp.int32, (SIZE, SIZE), 0) == SIZE - 1).astype(jnp.float32)
    heads_ref[0] = spread_ref[0:SIZE, :]

    def power(k, carry):
        head = heads_ref[k]
        scaled_ref[...] = terms_ref[0] * head
        left = [left_ref[8 * i:8 * i + 8, :] for i in range(TILES)]
        sums = [jnp.zeros((8, SIZE), jnp.float32) for _ in range(TILES)]
        for s in range(SIZE):
            factor = scaled_ref[s:s + 1, :]
            total = None
            for i in range(s // 8, TILES):
                part = spread_ref[s * SIZE + 8 * i:s * SIZE + 8 * i + 8, :]
                sums[i] = sums[i] + part * factor
                term = part * left[i]
                total = term if total is None else total + term
            product_ref[s:s + 1, :] = jnp.sum(total, axis=0, keepdims=True)
        after = jnp.minimum(k + 1, steps - 1)
        heads = jnp.concatenate(sums, axis=0) - terms_ref[1] * head
        @pl.when(k < steps - 1)
        def _():
            heads_ref[after] = heads
        product = product_ref[...]
        rows_ref[k] = product * terms_ref[2]
        note_ref[pl.ds(16 + k, 1), :] = product[0:1, :]
        new = product * terms_ref[0] - left_ref[...] * terms_ref[1]
        left_ref[...] = new
        note_ref[pl.ds(1 + k, 1), :] = jnp.sum(new * terms_ref[3], axis=0, keepdims=True)
        return carry

    lax.fori_loop(0, steps, power, 0)
    store = pltpu.make_async_copy(note_ref, far_note_ref, sem)
    store.start()
    store.wait()


def lateral_kernel(steps, slots, arrived_ref, far_note_ref, far_rows_ref, far_lateral_ref, far_notes_ref,
                   note_ref, rows_ref, lateral_ref, notes_ref, sems):
    opening = pltpu.make_async_copy(far_note_ref, note_ref, sems.at[2])
    opening.start()
    fetch = pltpu.make_async_copy(far_rows_ref, rows_ref, sems.at[0])
    fetch.start()
    sources = arrived_ref.shape[0] // (slots * steps)
    opening.wait()
    block = lax.broadcasted_iota(jnp.int32, (SIZE, sources), 0).astype(jnp.float32)
    select = [(note_ref[32 + k:33 + k, :] == block).astype(jnp.bfloat16) for k in range(slots)]
    for t in range(steps):
        total = None
        for k in range(slots):
            piece = arrived_ref[pl.ds(t * slots + k, sources, stride=slots * steps), :]
            high = piece.astype(jnp.bfloat16)
            low = (piece - high.astype(jnp.float32)).astype(jnp.bfloat16)
            for part in (high, low):
                term = jnp.dot(select[k], part, preferred_element_type=jnp.float32)
                total = term if total is None else total + term
        lateral_ref[t] = total.T
    store = pltpu.make_async_copy(lateral_ref, far_lateral_ref, sems.at[1])
    store.start()
    fetch.wait()
    sums = [jnp.zeros((8, SIZE), jnp.float32) for _ in range(steps)]
    for i in range(TILES):
        tile = slice(8 * i, 8 * i + 8)
        given = [lateral_ref[t, tile, :] for t in range(steps)]
        weight = [rows_ref[t, tile, :] for t in range(steps)]
        for t in range(steps):
            for j in range(t + 1):
                sums[t] = sums[t] + weight[t - j] * given[j]
    note = note_ref[0:32, :]
    series = [jnp.sum(part, axis=0, keepdims=True) for part in sums]
    whole = jnp.concatenate(
        [note[0:1]] + [note[1 + t:2 + t] + series[t] for t in range(steps)] + [note[1 + steps:]], axis=0)
    for d in range(notes_ref.shape[0]):
        notes_ref[d] = whole
    send = pltpu.make_async_copy(notes_ref, far_notes_ref, sems.at[3])
    send.start()
    send.wait()
    store.wait()


def local_kernel(steps, terms_ref, far_spread_ref, far_lateral_ref, flow_ref, spread_ref, lateral_ref, scaled_ref, sems):
    def fetch(j):
        where = (pl.ds(8 * j, 8), pl.ds(8 * j, SIZE - 8 * j))
        return pltpu.make_async_copy(far_spread_ref.at[where], spread_ref.at[where], sems.at[j])

    given = pltpu.make_async_copy(far_lateral_ref, lateral_ref, sems.at[TILES])
    given.start()
    for j in range(TILES):
        fetch(j).start()
    flow_ref[...] = terms_ref[3]
    given.wait()

    def step(t, first):
        flow = flow_ref[...]
        scaled_ref[...] = terms_ref[0] * flow + terms_ref[2] * lateral_ref[t]
        sums = [jnp.zeros((8, SIZE), jnp.float32) for _ in range(TILES)]
        for s in range(SIZE):
            if first and s % 8 == 0:
                fetch(s // 8).wait()
            factor = scaled_ref[s:s + 1, :]
            for i in range(s // 8, TILES):
                sums[i] = sums[i] + spread_ref[s, 8 * i:8 * i + 8, :] * factor
        flow_ref[...] = jnp.concatenate(sums, axis=0) - terms_ref[1] * flow

    step(0, True)

    def rest(t, carry):
        step(t, False)
        return carry

    lax.fori_loop(1, steps, rest, 0)


def chain_kernel(steps, notes_ref, flow_ref, far_heads_ref, lon_ref, out_ref, pad_ref, heads_ref, sem):
    fetch = pltpu.make_async_copy(far_heads_ref, heads_ref, sem)
    fetch.start()
    count = notes_ref.shape[0]
    me = lon_ref[0]
    row = lax.broadcasted_iota(jnp.int32, (16, SIZE), 0)
    zeros = jnp.zeros((16, SIZE), jnp.float32)
    for k in range(count):
        pad_ref[k, 0:16, :] = zeros
        pad_ref[k, 16:32, :] = notes_ref[k, 16:32, :]

    def inlet(k, series):
        link = jnp.broadcast_to(notes_ref[k, 15:16, :].astype(jnp.int32), (16, SIZE))
        coming = jnp.concatenate([gathered(series[0:8], link[0:8], 1), gathered(series[8:16], link[0:8], 1)], axis=0)
        coming = jnp.where(row <= steps, coming, 0.0)
        return notes_ref[k, 13:14, :] * coming + notes_ref[k, 14:15, :] * pltpu.roll(coming, 1, 0)

    def hop(k, series):
        entering = inlet(k, series)
        new = notes_ref[k, 0:16, :]
        for t in range(1, steps + 1):
            new = new + pad_ref[k, 16 - t:32 - t, :] * entering[t:t + 1, :]
        return new

    series = lax.fori_loop(1, me, hop, notes_ref[0, 0:16, :])
    entering = jnp.where(me > 0, inlet(me, series), 0.0)
    fetch.wait()
    flow = flow_ref[...]
    for t in range(1, steps + 1):
        flow = flow + heads_ref[steps - t] * entering[t:t + 1, :]
    out_ref[...] = flow.T


def body(runoff, cell_order, map_weights, dest_device, dest_block, initial_flow, musk_k, musk_x, down_reach,
         block_inverse, upstream_link):
    steps = runoff.shape[0]
    lat_count, lon_count = lax.axis_size("lat"), lax.axis_size("lon")
    devices = lat_count * lon_count
    lon_index = lax.axis_index("lon")
    my_index = lax.axis_index("lat") * lon_count + lon_index
    weights = map_weights.reshape(map_weights.shape[2:])
    sources, cells, reaches = weights.shape
    slots = 4
    targets = dest_device.reshape(devices, sources)
    me = my_index.reshape(1).astype(jnp.int32)
    outgoing = map_sources(cell_order.reshape(sources, cells), runoff, dest_device.reshape(devices * sources // 128, 128), me,
                           weights, devices, slots)
    arrived = lax.all_to_all(outgoing.reshape(devices, slots * steps, reaches), ("lat", "lon"),
                             split_axis=0, concat_axis=0, tiled=True)
    arrived = arrived.reshape(devices * slots * steps, reaches)

    vmem = pl.BlockSpec(memory_space=pltpu.VMEM)
    smem = pl.BlockSpec(memory_space=pltpu.SMEM)

    def params(mib):
        return pltpu.CompilerParams(vmem_limit_bytes=mib << 20)

    def near(x):
        return pltpu.with_memory_space_constraint(x, pltpu.VMEM)

    far = pl.BlockSpec(memory_space=pltpu.HBM)
    blocks = initial_flow.shape[2]
    plane = (reaches, blocks)
    moves = pltpu.SemaphoreType.DMA

    def made(*shape):
        return jax.ShapeDtypeStruct(shape, jnp.float32)

    spread, rows, heads, terms, note = pl.pallas_call(
        functools.partial(prepare_kernel, steps, slots),
        out_shape=[made(reaches * reaches, blocks), made(steps, *plane), made(steps, *plane), made(4, *plane),
                   pltpu.HBM((40, blocks), jnp.float32)],
        in_specs=[vmem] * 8 + [smem],
        out_specs=[vmem] * 4 + [far],
        scratch_shapes=[pltpu.VMEM((40, blocks), jnp.float32)] + [pltpu.VMEM(plane, jnp.float32)] * 3 + [moves],
        compiler_params=params(52),
        cost_estimate=pl.CostEstimate(flops=2 * 24 * blocks * reaches * reaches, bytes_accessed=20 << 20, transcendentals=0),
    )(
        block_inverse.reshape(blocks * reaches, reaches),
        musk_k.reshape(blocks, reaches),
        musk_x.reshape(blocks, reaches),
        down_reach.reshape(blocks, reaches),
        initial_flow.reshape(blocks, reaches),
        upstream_link.reshape(1, blocks),
        targets,
        dest_block.reshape(devices, sources),
        me,
    )
    lateral, notes = pl.pallas_call(
        functools.partial(lateral_kernel, steps, slots),
        out_shape=[pltpu.HBM((steps, *plane), jnp.float32), pltpu.HBM((lon_count, 32, blocks), jnp.float32)],
        in_specs=[vmem, far, far],
        out_specs=[far, far],
        scratch_shapes=[pltpu.VMEM((40, blocks), jnp.float32)] + [pltpu.VMEM((steps, *plane), jnp.float32)] * 2
        + [pltpu.VMEM((lon_count, 32, blocks), jnp.float32), moves((4,))],
        compiler_params=params(10),
    )(near(arrived), away(note), away(rows))
    notes = lax.all_to_all(notes, "lon", split_axis=0, concat_axis=0, tiled=True)
    flow = pl.pallas_call(
        functools.partial(local_kernel, steps),
        out_shape=made(*plane),
        in_specs=[vmem, far, far],
        out_specs=vmem,
        scratch_shapes=[pltpu.VMEM((reaches, *plane), jnp.float32), pltpu.VMEM((steps, *plane), jnp.float32),
                        pltpu.VMEM(plane, jnp.float32), moves((TILES + 1,))],
        compiler_params=params(52),
        cost_estimate=pl.CostEstimate(flops=2 * 12 * blocks * reaches * reaches, bytes_accessed=8 << 20, transcendentals=0),
    )(terms, away(spread.reshape(reaches, *plane)), away(lateral))
    result = pl.pallas_call(
        functools.partial(chain_kernel, steps),
        out_shape=made(blocks, reaches),
        in_specs=[vmem, vmem, far, smem],
        out_specs=vmem,
        scratch_shapes=[pltpu.VMEM((lon_count, 32, blocks), jnp.float32), pltpu.VMEM((steps, *plane), jnp.float32), moves],
        compiler_params=params(10),
    )(near(notes), flow, away(heads), lon_index.reshape(1).astype(jnp.int32))
    return result.reshape(initial_flow.shape)


def solution(mesh):
    return jax.shard_map(
        body,
        mesh=mesh,
        in_specs=(
            P(None, "lat", "lon"),
            P("lat", "lon", None),
            P("lat", "lon", None, None, None),
            P(),
            P(),
            P("lat", "lon", None, None),
            P("lat", "lon", None, None),
            P("lat", "lon", None, None),
            P("lat", "lon", None, None),
            P("lat", "lon", None, None, None),
            P("lat", "lon", None),
        ),
        out_specs=P("lat", "lon", None, None),
        check_vma=False,
    )
```

```python
import functools
import jax
import jax.numpy as jnp
from jax import lax
from jax.experimental import pallas as pl
from jax.experimental.pallas import tpu as pltpu
from jax.sharding import PartitionSpec as P

substep_seconds = 300.0

VREGS = 32
CHUNKS = 1
TOGETHER = 6

def gathered(x, index, axis):
    return jnp.take_along_axis(x, index, axis=axis, mode="promise_in_bounds")

def map_kernel(slots, far_order_ref, grid_ref, owners_ref, me_ref, weights_ref, out_ref,
               target_ref, order_ref, runoff_ref, pick_ref, held_ref, marks_ref, subs_ref, lanes_ref, counts_ref, sems):
    sources = weights_ref.shape[0]
    part = sources // CHUNKS
    def fetch(i):
        rows = pl.ds(i * part, part)
        return pltpu.make_async_copy(weights_ref.at[rows], held_ref.at[rows], sems.at[i])
    order_copy = pltpu.make_async_copy(far_order_ref, order_ref, sems.at[CHUNKS + 1])
    order_copy.start()
    per_device = weights_ref.shape[0] // 128
    first_row = me_ref[0] * per_device
    aligned = (first_row >> 3) << 3
    within = first_row - aligned
    target_copy = pltpu.make_async_copy(
        owners_ref.at[pl.ds(pl.multiple_of(aligned, 8), 8)], target_ref, sems.at[CHUNKS + 2])
    target_copy.start()
    grid_copy = pltpu.make_async_copy(grid_ref, runoff_ref, sems.at[CHUNKS])
    grid_copy.start()
    for i in range(CHUNKS):
        fetch(i).start()

    out_ref[...] = jnp.zeros_like(out_ref)
    def clear(d, carry):
        counts_ref[d] = 0
        return carry
    lax.fori_loop(0, counts_ref.shape[0], clear, 0)
    order_copy.wait()

    lane = lax.broadcasted_iota(jnp.int32, (8, 128), 1)
    sub = lax.broadcasted_iota(jnp.int32, (8, 128), 0)
    keys = []
    for v in range(VREGS):
        c = order_ref[pl.ds(8 * v, 8), :]
        keys.append(((c & 127) << 8) | (((c >> 8) & 7) << 5) | (((c >> 7) & 1) << 4) | (c >> 11))

    def flips(q):
        if q == 0 or q >= 15:
            return [None] * VREGS
        if q < 5:
            return [bool((v >> q) & 1) for v in range(VREGS)]
        bit = (sub >> (q - 5)) & 1 if q < 8 else (lane >> (q - 8)) & 1
        return [bit] * VREGS

    def as_word(flip):
        if flip is None or flip is False:
            return None
        if flip is True:
            return -1
        return -flip

    pair = 0
    undo = []
    for q in range(1, 16):
        before, now = flips(q - 1), flips(q)
        for v in range(VREGS):
            a, b = as_word(before[v]), as_word(now[v])
            if a is None and b is None:
                continue
            if isinstance(a, int) and isinstance(b, int):
                continue
            word = b if a is None else (a if b is None else a ^ b)
            keys[v] = keys[v] ^ word
        lane_bits = [k for k in range(q - 1, 7, -1)]
        sub_bits = [k for k in range(min(q - 1, 7), 4, -1)]
        for bits, axis, place, low, ref in ((lane_bits, 1, lane, 8, lanes_ref), (sub_bits, 0, sub, 5, subs_ref)):
            if not bits:
                continue
            marks = [[] for _ in range(VREGS)]
            for k in bits:
                d = 1 << (k - low)
                partner = place ^ d
                upper = (place & d) != 0
                for v in range(VREGS):
                    other = gathered(keys[v], partner, axis)
                    new = jnp.where(upper, jnp.maximum(keys[v], other), jnp.minimum(keys[v], other))
                    marks[v].append((new != keys[v], partner))
                    keys[v] = new
            row = (q - 9) if axis == 1 else (q - 6)
            index = [place] * VREGS
            for n in reversed(range(len(bits))):
                for v in range(VREGS):
                    mark, partner = marks[v][n]
                    other = partner if index[v] is place else gathered(index[v], partner, axis)
                    index[v] = jnp.where(mark, other, index[v])
            for v in range(VREGS):
                ref[row * VREGS + v] = index[v]
        pairs = []
        for k in range(min(q - 1, 4), -1, -1):
            for v in range(VREGS):
                if v & (1 << k):
                    continue
                w = v | (1 << k)
                a, b = keys[v], keys[w]
                marks_ref[pair] = (a > b).astype(jnp.int32)
                keys[v], keys[w] = jnp.minimum(a, b), jnp.maximum(a, b)
                pairs.append((pair, v, w))
                pair += 1
        undo.append((q, pairs))

    planes = runoff_ref.shape[0] // 2
    grid_copy.wait()

    def several(g, carry):
        first = g * TOGETHER
        xs = []
        for n in range(TOGETHER):
            p = first + n
            low = (runoff_ref[p].astype(jnp.float32) * 4096.0).astype(jnp.int32)
            high = (runoff_ref[p + planes].astype(jnp.float32) * 4096.0).astype(jnp.int32)
            both = low | (high << 16)
            xs.append([both[8 * r:8 * r + 8, 128 * h:128 * h + 128] for h in range(2) for r in range(16)])
        for q, pairs in reversed(undo):
            for base in range(0, TOGETHER, 2):
                some = xs[base:base + 2]
                for at, v, w in reversed(pairs):
                    mark = marks_ref[at] != 0
                    for x in some:
                        x[v], x[w] = jnp.where(mark, x[w], x[v]), jnp.where(mark, x[v], x[w])
                for v in range(VREGS):
                    if q >= 6:
                        index = subs_ref[(q - 6) * VREGS + v]
                        for x in some:
                            x[v] = gathered(x[v], index, 0)
            if q >= 9:
                for v in range(VREGS):
                    index = lanes_ref[(q - 9) * VREGS + v]
                    for x in xs:
                        x[v] = gathered(x[v], index, 1)
        scale = 1.0 / 4096.0
        for n, x in enumerate(xs):
            for v in range(VREGS):
                p = 128 * v + first + n
                pick_ref[pl.ds(p, 8, stride=16), :] = (x[v] & 0xFFFF).astype(jnp.float32) * scale
                pick_ref[pl.ds(p + planes, 8, stride=16), :] = (x[v] >> 16).astype(jnp.float32) * scale
        return carry

    lax.fori_loop(0, planes // TOGETHER, several, 0)

    target_copy.wait()
    steps = 2 * planes
    unroll = 256
    for i in range(CHUNKS):
        fetch(i).wait()
        def group(g, carry):
            for u in range(0, unroll, 2):
                s = i * part + g * unroll + u
                rows = pick_ref[pl.ds(pl.multiple_of(s * 16, 32), 32), :].astype(jnp.bfloat16)
                none = jnp.zeros((16, 128), jnp.bfloat16)
                lhs = jnp.concatenate([jnp.concatenate([rows[:16], none], 1), jnp.concatenate([none, rows[16:]], 1)], 0)
                both = jnp.dot(lhs, held_ref[pl.ds(s, 2)].reshape(256, 128), preferred_element_type=jnp.float32)
                for n in range(2):
                    d = target_ref[within + ((s + n) >> 7), (s + n) & 127]
                    k = counts_ref[d]
                    counts_ref[d] = k + 1
                    out_ref[pl.ds(d * (slots * steps) + k, steps, stride=slots), :] = both[16 * n:16 * n + steps]
            return carry
        lax.fori_loop(0, part // unroll, group, 0)


def away(x):
    return pltpu.with_memory_space_constraint(x, pltpu.HBM)


def map_sources(order, runoff, owners, me, weights, devices, slots):
    steps = runoff.shape[0]
    sources, cells, reaches = weights.shape
    vmem = pl.BlockSpec(memory_space=pltpu.VMEM)
    far = pl.BlockSpec(memory_space=pltpu.HBM)
    return pl.pallas_call(
        functools.partial(map_kernel, slots),
        out_shape=jax.ShapeDtypeStruct((devices * slots * steps, reaches), jnp.float32),
        in_specs=[far, far, far, pl.BlockSpec(memory_space=pltpu.SMEM), far],
        out_specs=vmem,
        scratch_shapes=[
            pltpu.SMEM((8, 128), jnp.int32),
            pltpu.VMEM(order.shape, order.dtype),
            pltpu.VMEM(runoff.shape, runoff.dtype),
            pltpu.VMEM((sources * 16, cells), jnp.float32),
            pltpu.VMEM(weights.shape, weights.dtype),
            pltpu.VMEM((1040, 8, 128), jnp.int32),
            pltpu.VMEM((10 * VREGS, 8, 128), jnp.int32),
            pltpu.VMEM((7 * VREGS, 8, 128), jnp.int32),
            pltpu.SMEM((devices,), jnp.int32),
            pltpu.SemaphoreType.DMA((CHUNKS + 3,)),
        ],
        compiler_params=pltpu.CompilerParams(vmem_limit_bytes=52 << 20),
    )(away(order), away(runoff), away(owners), me, away(weights))


def coefficients(travel, weighting):
    half = 0.5 * substep_seconds
    denom = travel * (1.0 - weighting) + half
    first = (half - travel * weighting) / denom
    second = (half + travel * weighting) / denom
    third = (travel * (1.0 - weighting) - half) / denom
    return first, second, third


TILES = 16
SIZE = 128


def prepare_kernel(steps, slots, inverse_ref, travel_ref, weighting_ref, drains_ref, flow_ref, links_ref,
                   targets_ref, blocks_ref, me_ref, spread_ref, rows_ref, heads_ref, terms_ref, far_note_ref,
                   note_ref, left_ref, scaled_ref, product_ref, sem):
    first, second, third = coefficients(travel_ref[...], weighting_ref[...])
    drains = drains_ref[...]
    nearest = jnp.minimum(drains, SIZE - 1)
    below = jnp.concatenate(
        [gathered(second[8 * i:8 * i + 8], nearest[8 * i:8 * i + 8], 1) for i in range(TILES)], axis=0)
    below = jnp.where(drains < SIZE, below, 0.0)
    ratio = below / first
    terms_ref[0] = (ratio + third).T
    terms_ref[1] = ratio.T
    terms_ref[2] = (first + second).T
    terms_ref[3] = flow_ref[...].T
    note_ref[...] = jnp.zeros_like(note_ref)
    note_ref[0:1, :] = terms_ref[3, SIZE - 1:SIZE, :]
    note_ref[13:14, :] = first.T[0:1, :]
    note_ref[14:15, :] = second.T[0:1, :]
    note_ref[15:16, :] = links_ref[...].astype(jnp.float32)

    hits = targets_ref[...] == me_ref[0]
    sources = hits.shape[1]
    order = lax.broadcasted_iota(jnp.int32, (sources, sources), 0)
    later = (order <= lax.broadcasted_iota(jnp.int32, (sources, sources), 1)).astype(jnp.bfloat16)
    place = jnp.dot(hits.astype(jnp.bfloat16), later, preferred_element_type=jnp.float32)
    numbers = blocks_ref[...].astype(jnp.float32) + 1.0
    for k in range(slots):
        here = hits & (place == k + 1.0)
        named = jnp.sum(jnp.where(here, numbers, 0.0), axis=1, keepdims=True) - 1.0
        note_ref[32 + k:33 + k, :] = jnp.broadcast_to(named, (SIZE, SIZE)).T[0:1, :]

    def turned(g, carry):
        for u in range(4):
            r = g * 4 + u
            spread_ref[pl.ds(r, SIZE, stride=SIZE), :] = inverse_ref[pl.ds(r, SIZE, stride=SIZE), :].T
        return carry

    lax.fori_loop(0, SIZE // 4, turned, 0)

    left_ref[...] = (lax.broadcasted_iota(jnp.int32, (SIZE, SIZE), 0) == SIZE - 1).astype(jnp.float32)
    heads_ref[0] = spread_ref[0:SIZE, :]

    def power(k, carry):
        head = heads_ref[k]
        scaled_ref[...] = terms_ref[0] * head
        left = [left_ref[8 * i:8 * i + 8, :] for i in range(TILES)]
        sums = [jnp.zeros((8, SIZE), jnp.float32) for _ in range(TILES)]
        for s in range(SIZE):
            factor = scaled_ref[s:s + 1, :]
            total = None
            for i in range(s // 8, TILES):
                part = spread_ref[s * SIZE + 8 * i:s * SIZE + 8 * i + 8, :]
                sums[i] = sums[i] + part * factor
                term = part * left[i]
                total = term if total is None else total + term
            product_ref[s:s + 1, :] = jnp.sum(total, axis=0, keepdims=True)
        after = jnp.minimum(k + 1, steps - 1)
        heads = jnp.concatenate(sums, axis=0) - terms_ref[1] * head
        @pl.when(k < steps - 1)
        def _():
            heads_ref[after] = heads
        product = product_ref[...]
        rows_ref[k] = product * terms_ref[2]
        note_ref[pl.ds(16 + k, 1), :] = product[0:1, :]
        new = product * terms_ref[0] - left_ref[...] * terms_ref[1]
        left_ref[...] = new
        note_ref[pl.ds(1 + k, 1), :] = jnp.sum(new * terms_ref[3], axis=0, keepdims=True)
        return carry

    lax.fori_loop(0, steps, power, 0)
    store = pltpu.make_async_copy(note_ref, far_note_ref, sem)
    store.start()
    store.wait()


def lateral_kernel(steps, slots, arrived_ref, far_note_ref, far_rows_ref, far_lateral_ref, far_notes_ref,
                   note_ref, rows_ref, lateral_ref, notes_ref, sems):
    opening = pltpu.make_async_copy(far_note_ref, note_ref, sems.at[2])
    opening.start()
    fetch = pltpu.make_async_copy(far_rows_ref, rows_ref, sems.at[0])
    fetch.start()
    sources = arrived_ref.shape[0] // (slots * steps)
    opening.wait()
    block = lax.broadcasted_iota(jnp.int32, (SIZE, sources), 0).astype(jnp.float32)
    select = [(note_ref[32 + k:33 + k, :] == block).astype(jnp.bfloat16) for k in range(slots)]
    for t in range(steps):
        total = None
        for k in range(slots):
            piece = arrived_ref[pl.ds(t * slots + k, sources, stride=slots * steps), :]
            high = piece.astype(jnp.bfloat16)
            low = (piece - high.astype(jnp.float32)).astype(jnp.bfloat16)
            for part in (high, low):
                term = jnp.dot(select[k], part, preferred_element_type=jnp.float32)
                total = term if total is None else total + term
        lateral_ref[t] = total.T
    store = pltpu.make_async_copy(lateral_ref, far_lateral_ref, sems.at[1])
    store.start()
    fetch.wait()
    sums = [jnp.zeros((8, SIZE), jnp.float32) for _ in range(steps)]
    for i in range(TILES):
        tile = slice(8 * i, 8 * i + 8)
        given = [lateral_ref[t, tile, :] for t in range(steps)]
        weight = [rows_ref[t, tile, :] for t in range(steps)]
        for t in range(steps):
            for j in range(t + 1):
                sums[t] = sums[t] + weight[t - j] * given[j]
    note = note_ref[0:32, :]
    series = [jnp.sum(part, axis=0, keepdims=True) for part in sums]
    whole = jnp.concatenate(
        [note[0:1]] + [note[1 + t:2 + t] + series[t] for t in range(steps)] + [note[1 + steps:]], axis=0)
    for d in range(notes_ref.shape[0]):
        notes_ref[d] = whole
    send = pltpu.make_async_copy(notes_ref, far_notes_ref, sems.at[3])
    send.start()
    send.wait()
    store.wait()


def local_kernel(steps, terms_ref, far_spread_ref, far_lateral_ref, flow_ref, spread_ref, lateral_ref, scaled_ref, sems):
    def fetch(j):
        where = (pl.ds(8 * j, 8), pl.ds(8 * j, SIZE - 8 * j))
        return pltpu.make_async_copy(far_spread_ref.at[where], spread_ref.at[where], sems.at[j])

    given = pltpu.make_async_copy(far_lateral_ref, lateral_ref, sems.at[TILES])
    given.start()
    for j in range(TILES):
        fetch(j).start()
    flow_ref[...] = terms_ref[3]
    given.wait()

    def step(t, first):
        flow = flow_ref[...]
        scaled_ref[...] = terms_ref[0] * flow + terms_ref[2] * lateral_ref[t]
        sums = [jnp.zeros((8, SIZE), jnp.float32) for _ in range(TILES)]
        for s in range(SIZE):
            if first and s % 8 == 0:
                fetch(s // 8).wait()
            factor = scaled_ref[s:s + 1, :]
            for i in range(s // 8, TILES):
                sums[i] = sums[i] + spread_ref[s, 8 * i:8 * i + 8, :] * factor
        flow_ref[...] = jnp.concatenate(sums, axis=0) - terms_ref[1] * flow

    step(0, True)

    def rest(t, carry):
        step(t, False)
        return carry

    lax.fori_loop(1, steps, rest, 0)


def chain_kernel(steps, notes_ref, flow_ref, far_heads_ref, lon_ref, out_ref, pad_ref, heads_ref, sem):
    fetch = pltpu.make_async_copy(far_heads_ref, heads_ref, sem)
    fetch.start()
    count = notes_ref.shape[0]
    me = lon_ref[0]
    row = lax.broadcasted_iota(jnp.int32, (16, SIZE), 0)
    zeros = jnp.zeros((16, SIZE), jnp.float32)
    for k in range(count):
        pad_ref[k, 0:16, :] = zeros
        pad_ref[k, 16:32, :] = notes_ref[k, 16:32, :]

    def inlet(k, series):
        link = jnp.broadcast_to(notes_ref[k, 15:16, :].astype(jnp.int32), (16, SIZE))
        coming = jnp.concatenate([gathered(series[0:8], link[0:8], 1), gathered(series[8:16], link[0:8], 1)], axis=0)
        coming = jnp.where(row <= steps, coming, 0.0)
        return notes_ref[k, 13:14, :] * coming + notes_ref[k, 14:15, :] * pltpu.roll(coming, 1, 0)

    def hop(k, series):
        entering = inlet(k, series)
        new = notes_ref[k, 0:16, :]
        for t in range(1, steps + 1):
            new = new + pad_ref[k, 16 - t:32 - t, :] * entering[t:t + 1, :]
        return new

    series = lax.fori_loop(1, me, hop, notes_ref[0, 0:16, :])
    entering = jnp.where(me > 0, inlet(me, series), 0.0)
    fetch.wait()
    flow = flow_ref[...]
    for t in range(1, steps + 1):
        flow = flow + heads_ref[steps - t] * entering[t:t + 1, :]
    out_ref[...] = flow.T


def body(runoff, cell_order, map_weights, dest_device, dest_block, initial_flow, musk_k, musk_x, down_reach,
         block_inverse, upstream_link):
    steps = runoff.shape[0]
    lat_count, lon_count = lax.axis_size("lat"), lax.axis_size("lon")
    devices = lat_count * lon_count
    lon_index = lax.axis_index("lon")
    my_index = lax.axis_index("lat") * lon_count + lon_index
    weights = map_weights.reshape(map_weights.shape[2:])
    sources, cells, reaches = weights.shape
    slots = 4
    targets = dest_device.reshape(devices, sources)
    me = my_index.reshape(1).astype(jnp.int32)
    outgoing = map_sources(cell_order.reshape(sources, cells), runoff, dest_device.reshape(devices * sources // 128, 128), me,
                           weights, devices, slots)
    arrived = lax.all_to_all(outgoing.reshape(devices, slots * steps, reaches), ("lat", "lon"),
                             split_axis=0, concat_axis=0, tiled=True)
    arrived = arrived.reshape(devices * slots * steps, reaches)

    vmem = pl.BlockSpec(memory_space=pltpu.VMEM)
    smem = pl.BlockSpec(memory_space=pltpu.SMEM)

    def params(mib):
        return pltpu.CompilerParams(vmem_limit_bytes=mib << 20)

    def near(x):
        return pltpu.with_memory_space_constraint(x, pltpu.VMEM)

    far = pl.BlockSpec(memory_space=pltpu.HBM)
    blocks = initial_flow.shape[2]
    plane = (reaches, blocks)
    moves = pltpu.SemaphoreType.DMA

    def made(*shape):
        return jax.ShapeDtypeStruct(shape, jnp.float32)

    spread, rows, heads, terms, note = pl.pallas_call(
        functools.partial(prepare_kernel, steps, slots),
        out_shape=[made(reaches * reaches, blocks), made(steps, *plane), made(steps, *plane), made(4, *plane),
                   pltpu.HBM((40, blocks), jnp.float32)],
        in_specs=[vmem] * 8 + [smem],
        out_specs=[vmem] * 4 + [far],
        scratch_shapes=[pltpu.VMEM((40, blocks), jnp.float32)] + [pltpu.VMEM(plane, jnp.float32)] * 3 + [moves],
        compiler_params=params(52),
        cost_estimate=pl.CostEstimate(flops=2 * 24 * blocks * reaches * reaches, bytes_accessed=20 << 20, transcendentals=0),
    )(
        block_inverse.reshape(blocks * reaches, reaches),
        musk_k.reshape(blocks, reaches),
        musk_x.reshape(blocks, reaches),
        down_reach.reshape(blocks, reaches),
        initial_flow.reshape(blocks, reaches),
        upstream_link.reshape(1, blocks),
        targets,
        dest_block.reshape(devices, sources),
        me,
    )
    lateral, notes = pl.pallas_call(
        functools.partial(lateral_kernel, steps, slots),
        out_shape=[pltpu.HBM((steps, *plane), jnp.float32), pltpu.HBM((lon_count, 32, blocks), jnp.float32)],
        in_specs=[vmem, far, far],
        out_specs=[far, far],
        scratch_shapes=[pltpu.VMEM((40, blocks), jnp.float32)] + [pltpu.VMEM((steps, *plane), jnp.float32)] * 2
        + [pltpu.VMEM((lon_count, 32, blocks), jnp.float32), moves((4,))],
        compiler_params=params(10),
    )(near(arrived), away(note), away(rows))
    notes = lax.all_to_all(notes, "lon", split_axis=0, concat_axis=0, tiled=True)
    flow = pl.pallas_call(
        functools.partial(local_kernel, steps),
        out_shape=made(*plane),
        in_specs=[vmem, far, far],
        out_specs=vmem,
        scratch_shapes=[pltpu.VMEM((reaches, *plane), jnp.float32), pltpu.VMEM((steps, *plane), jnp.float32),
                        pltpu.VMEM(plane, jnp.float32), moves((TILES + 1,))],
        compiler_params=params(52),
        cost_estimate=pl.CostEstimate(flops=2 * 12 * blocks * reaches * reaches, bytes_accessed=8 << 20, transcendentals=0),
    )(terms, away(spread.reshape(reaches, *plane)), away(lateral))
    result = pl.pallas_call(
        functools.partial(chain_kernel, steps),
        out_shape=made(blocks, reaches),
        in_specs=[vmem, vmem, far, smem],
        out_specs=vmem,
        scratch_shapes=[pltpu.VMEM((lon_count, 32, blocks), jnp.float32), pltpu.VMEM((steps, *plane), jnp.float32), moves],
        compiler_params=params(10),
    )(near(notes), flow, away(heads), lon_index.reshape(1).astype(jnp.int32))
    return result.reshape(initial_flow.shape)


def solution(mesh):
    return jax.shard_map(
        body,
        mesh=mesh,
        in_specs=(
            P(None, "lat", "lon"),
            P("lat", "lon", None),
            P("lat", "lon", None, None, None),
            P(),
            P(),
            P("lat", "lon", None, None),
            P("lat", "lon", None, None),
            P("lat", "lon", None, None),
            P("lat", "lon", None, None),
            P("lat", "lon", None, None, None),
            P("lat", "lon", None),
        ),
        out_specs=P("lat", "lon", None, None),
        check_vma=False,
    )
```
